32 devices in a mesh: gx: 16 (over z, x, core), gy: 2 (over y).
Axes of the slice: x: 2, y: 2, z: 4, core: 2. Of those that a mesh axis runs over, the one named last changes fastest.
Arguments:
- features: bfloat16 [96, 256, 256], P('gy', 'gx'), may hold values from -6 to 6
- first_filter: bfloat16 [256, 3, 3, 256], P('gy'), may hold values from -0.125 to 0.125
- second_filter: bfloat16 [256, 3, 3, 256], P('gy'), may hold values from -0.125 to 0.125
- cotangent: bfloat16 [256, 256, 96], P('gy', 'gx'), may hold values from -6 to 6
Outputs:
- output: bfloat16 [256, 256, 96], P('gy', 'gx')
- input_grad: bfloat16 [96, 256, 256], P('gy', 'gx')
- first_grad: float32 [256, 3, 3, 256], P('gy')
- second_grad: float32 [256, 3, 3, 256], P('gy')
The draws below stay inside these ranges and needn't reach their ends.
All inputs are finite; a program needn't handle non-finite values.
Results may differ from the reference program's by a relative error of at most 0.0059.
Values may be sent and summed in bfloat16 or wider, within the bound.
No kernel may reach another device: no remote copies, remote signals or barrier semaphores. Data moves between devices by JAX's collectives and lax.ppermute only.
A program may use at most 128 MiB of HBM per device.

```python
import math
import jax
import jax.numpy as jnp
from jax import lax

C = 256
ROWS = 96
COLS = 256


def steps_of(rng, shape, shards, low, top_value):
    level = 1.0
    for position, blocks in shards:
        draws = jax.random.uniform(jax.random.fold_in(jax.random.fold_in(rng, 6), position), (blocks,), jnp.float32, low / len(shards), top_value / len(shards))
        level = level * jnp.repeat(jnp.exp(draws), shape[position] // blocks).reshape((-1,) + (1,) * (len(shape) - 1 - position))
    return level


def normal_values(key, shape, scale, most, cuts=(), kind=jnp.bfloat16):
    entries = jax.random.normal(key, shape, jnp.float32) * scale
    if len(cuts) > 0:
        entries = steps_of(key, shape, cuts, -0.22, 0.18) * entries
    return jnp.clip(entries, min=-most, max=most).astype(kind)


def setup_inputs(seed: int = 0) -> dict:
    key_of = jax.random.split(jax.random.key(seed), 5)
    return {
        "features": normal_values(key_of[0], (ROWS, COLS, C), 1.0, 6.0, ((0, 2), (1, 16))),
        "first_filter": normal_values(key_of[1], (C, 3, 3, C), (9 * C) ** -0.5, 0.125, ((0, 2),)),
        "second_filter": normal_values(key_of[2], (C, 3, 3, C), (9 * C) ** -0.5, 0.125, ((0, 2),)),
        "cotangent": normal_values(key_of[3], (C, COLS, ROWS), 1.0, 6.0, ((0, 2), (1, 16))),
    }


def silu_parts(pre):
    sigma = jax.nn.sigmoid(pre)
    return (pre * sigma, sigma * (1.0 + pre * (1.0 - sigma)))

def conv_taps(padded, weight, height, width):
    total = jnp.zeros((height * width, weight.shape[3]), jnp.float32)
    for i in range(3):
        for j in range(3):
            window = padded[i:i + height, j:j + width, :].reshape(height * width, padded.shape[2])
            total = total + jnp.dot(window, weight[i, j], preferred_element_type=jnp.float32)
    return total.reshape(height, width, weight.shape[3])

def flipped(weight):
    return jnp.transpose(weight[::-1, ::-1], (0, 1, 3, 2))

def filter_grad(padded, grad, height, width):
    flat_grad = grad.reshape(height * width, grad.shape[2])
    tap_list = []
    for i in range(3):
        for j in range(3):
            window = padded[i:i + height, j:j + width, :].reshape(height * width, padded.shape[2])
            tap_list.append(lax.dot_general(window, flat_grad, (((0,), (0,)), ((), ())), preferred_element_type=jnp.float32))
    return jnp.stack(tap_list).reshape(3, 3, padded.shape[2], grad.shape[2])

def pad_both(field):
    return jnp.pad(field, ((1, 1), (1, 1), (0, 0)))

def reference(features, first_filter, second_filter, cotangent):
    height = features.shape[0]
    width = features.shape[1]
    scale_factor = 1.0 / math.sqrt(height * width)
    first_taps = jnp.transpose(first_filter, (1, 2, 3, 0))
    second_taps = jnp.transpose(second_filter, (1, 2, 3, 0))
    cot_map = jnp.transpose(cotangent, (2, 1, 0))
    feat_padded = pad_both(features)
    first_pre = conv_taps(feat_padded, first_taps, height, width)
    first_act, first_slope = silu_parts(first_pre)
    hidden = first_act.astype(jnp.bfloat16)
    hidden_padded = pad_both(hidden)
    second_pre = conv_taps(hidden_padded, second_taps, height, width)
    second_act, second_slope = silu_parts(second_pre)
    output = jnp.transpose(second_act.astype(jnp.bfloat16), (2, 1, 0))
    outer_grad = (cot_map.astype(jnp.float32) * second_slope).astype(jnp.bfloat16)
    second_grad = filter_grad(hidden_padded, outer_grad, height, width) * scale_factor
    hidden_grad = conv_taps(pad_both(outer_grad), flipped(second_taps), height, width)
    inner_grad = (hidden_grad * first_slope).astype(jnp.bfloat16)
    first_grad = filter_grad(feat_padded, inner_grad, height, width) * scale_factor
    input_grad = conv_taps(pad_both(inner_grad), flipped(first_taps), height, width).astype(jnp.bfloat16)
    return (output, input_grad, jnp.transpose(first_grad, (3, 0, 1, 2)), jnp.transpose(second_grad, (3, 0, 1, 2)))
```

```python
import functools
import math

import jax
import jax.numpy as jnp
from jax import lax
from jax.experimental import pallas as pl
from jax.experimental.pallas import tpu as pltpu
from jax.sharding import PartitionSpec as P

F32, BF16 = jnp.float32, jnp.bfloat16
OFF = 8
VMEM_LIMIT = 56 * 1024 * 1024
NT = (((1,), (1,)), ((), ()))


def call(kernel, outs, args, scratch=(), flops=0, smem_args=1):
    specs = [pl.BlockSpec(memory_space=pltpu.SMEM)] * smem_args
    specs += [pl.BlockSpec(memory_space=pltpu.VMEM)] * (len(args) - smem_args)
    nbytes = sum(a.size * a.dtype.itemsize for a in args[smem_args:])
    nbytes += sum(math.prod(s) * jnp.dtype(t).itemsize for s, t in outs)
    return pl.pallas_call(
        kernel,
        out_shape=[jax.ShapeDtypeStruct(s, t) for s, t in outs],
        in_specs=specs,
        out_specs=[pl.BlockSpec(memory_space=pltpu.VMEM)] * len(outs),
        scratch_shapes=list(scratch),
        compiler_params=pltpu.CompilerParams(vmem_limit_bytes=VMEM_LIMIT),
        cost_estimate=pl.CostEstimate(flops=flops, bytes_accessed=nbytes, transcendentals=0),
    )(*args)


def silu_parts(pre):
    sigma = 1.0 / (1.0 + jnp.exp(-pre))
    return pre * sigma, sigma * (1.0 + pre * (1.0 - sigma))


def row_mask(first, rows, total):
    at = lax.broadcasted_iota(jnp.int32, (rows, 1), 0) + (first - OFF)
    return (at >= 0) & (at < total)


def shifted_rows(x):
    n = x.shape[0]
    return pltpu.roll(x, 1, 0), x, pltpu.roll(x, n - 1, 0)


def fill_shifted(buf, c, x):
    ch = x.shape[1]
    for i, part in enumerate(shifted_rows(x)):
        buf[c, :, i * ch : (i + 1) * ch] = part.astype(BF16)


def conv_chunk(buf, w, c0, n, backward):
    rows, ch = buf.shape[1], w.shape[1]
    total = None
    for j in range(3):
        for i in range(3):
            lhs = buf[c0 + j : c0 + j + n, :, i * ch : (i + 1) * ch].reshape(n * rows, ch)
            if backward:
                term = jnp.dot(lhs, w[(2 - j) * 3 + (2 - i)], preferred_element_type=F32)
            else:
                term = lax.dot_general(lhs, w[j * 3 + i], NT, preferred_element_type=F32)
            total = term if total is None else total + term
    return total.reshape(n, rows, ch)


def chunks(total, most):
    parts = -(-total // most)
    base, extra = divmod(total, parts)
    out, at = [], 0
    for p in range(parts):
        n = base + (p < extra)
        out.append((at, n))
        at += n
    return out


def assemble_filter(w, own, pieces, iy, core, ny):
    co = own.shape[1]
    half = co // 2
    w[:, pl.ds(pl.multiple_of(iy * co, co), co), :] = own[...]
    for d in range(1, ny):
        src = lax.rem(iy - d + ny, ny)
        mine, other = pieces
        at = pl.multiple_of(src * co + core * half, half)
        w[:, pl.ds(at, half), :] = mine[d - 1]
        at = pl.multiple_of(src * co + (1 - core) * half, half)
        w[:, pl.ds(at, half), :] = other[d - 1]


def conv1_kernel(dims, where, ft, left, right, up, down, own, mine, other, hidden, slope, fbuf, w, buf):
    ny, hl, wl, height, width = dims
    iy, ix = where[0], where[1]
    rows = fbuf.shape[1]
    ok = row_mask(iy * hl, rows, height)
    for c in range(wl + 8):
        mid = left[c] if c < 4 else (ft[c - 4] if c < wl + 4 else right[c - wl - 4])
        x = jnp.concatenate([up[c].astype(F32), mid.astype(F32), down[c].astype(F32)], axis=0)
        x = jnp.where(ok, x, 0.0)
        fbuf[c] = x.astype(BF16)
        fill_shifted(buf, c, x)
    assemble_filter(w, own, (mine, other), iy, ix % 2, ny)
    for c0, n in chunks(wl + 6, 11):
        pre = conv_chunk(buf, w, c0, n, False)
        for q in range(n):
            c = c0 + q
            col = ix * wl + c - 3
            act, grad = silu_parts(pre[q])
            inside = ok & (col >= 0) & (col < width)
            hidden[c] = jnp.where(inside, act, 0.0).astype(BF16)
            if 2 <= c < wl + 4:
                slope[c - 2] = jnp.where(inside, grad, 0.0)


def conv2_kernel(dims, where, hidden, own, mine, other, act_out, slope, w, buf):
    ny, hl, wl, height, width = dims
    iy, ix = where[0], where[1]
    rows = hidden.shape[1]
    ok = row_mask(iy * hl, rows, height)
    for c in range(wl + 6):
        fill_shifted(buf, c, hidden[c].astype(F32))
    assemble_filter(w, own, (mine, other), iy, ix % 2, ny)
    for c0, n in chunks(wl + 4, 10):
        pre = conv_chunk(buf, w, c0, n, False)
        for q in range(n):
            c = c0 + q
            col = ix * wl + c - 2
            act, grad = silu_parts(pre[q])
            inside = ok & (col >= 0) & (col < width)
            slope[c] = jnp.where(inside, grad, 0.0)
            if 2 <= c < wl + 2:
                act_out[c - 2] = act[OFF : OFF + hl].astype(BF16)


def own_rows(rows, hl):
    at = lax.broadcasted_iota(jnp.int32, (rows, 1), 0)
    return (at >= OFF) & (at < OFF + hl)


def filter_grad(where, buf, first, grad_t, wl, keep, send):
    core = where[1] % 2
    rows, ch = buf.shape[1], grad_t.shape[0]
    half = ch // 2
    for j in range(3):
        for i in range(3):
            rhs = buf[first + j : first + j + wl, :, i * ch : (i + 1) * ch].reshape(wl * rows, ch)
            g = jnp.dot(grad_t, rhs, preferred_element_type=F32)
            low, high = g[:, :half], g[:, half:]
            keep[j * 3 + i] = jnp.where(core == 0, low, high)
            send[j * 3 + i] = jnp.where(core == 0, high, low).astype(BF16)


def outer_kernel(dims, count, where, hidden, slope, *refs):
    cots, (outer, keep, send, buf, gt) = refs[:count], refs[count:]
    ny, hl, wl, height, width = dims
    iy = where[0]
    rows = hidden.shape[1]
    own = own_rows(rows, hl)
    for c in range(wl + 2):
        fill_shifted(buf, c, hidden[c + 2].astype(F32))
    for c in range(wl + 4):
        parts = [ref[c].astype(F32) for ref in cots]
        if len(parts) == 2:
            a, b = parts
            parts = [jnp.where(iy == 0, a, b), jnp.where(iy == 0, b, a)]
        outer[c] = (jnp.concatenate(parts, axis=1) * slope[c]).astype(BF16)
    for c in range(wl):
        val = jnp.where(own, outer[c + 2].astype(F32), 0.0)
        gt[:, c * rows : (c + 1) * rows] = val.T.astype(BF16)
    filter_grad(where, buf, 0, gt[...], wl, keep, send)


def inner_kernel(dims, where, outer, own, mine, other, slope, fbuf, inner, keep, send, w, buf, gt):
    ny, hl, wl, height, width = dims
    iy, ix = where[0], where[1]
    rows = fbuf.shape[1]
    for c in range(wl + 4):
        fill_shifted(buf, c, outer[c].astype(F32))
    assemble_filter(w, own, (mine, other), iy, ix % 2, ny)
    mine_rows = own_rows(rows, hl)
    for c0, n in chunks(wl + 2, 9):
        grad = conv_chunk(buf, w, c0, n, True)
        for q in range(n):
            c = c0 + q
            val = grad[q] * slope[c]
            inner[c] = val.astype(BF16)
            if 1 <= c < wl + 1:
                val = jnp.where(mine_rows, val, 0.0)
                gt[:, (c - 1) * rows : c * rows] = val.T.astype(BF16)
    for c in range(wl + 2):
        fill_shifted(buf, c, fbuf[c + 3].astype(F32))
    filter_grad(where, buf, 0, gt[...], wl, keep, send)


def input_kernel(dims, where, inner, own, mine, other, out, w, buf):
    ny, hl, wl, height, width = dims
    iy, ix = where[0], where[1]
    for c in range(wl + 2):
        fill_shifted(buf, c, inner[c].astype(F32))
    assemble_filter(w, own, (mine, other), iy, ix % 2, ny)
    for c0, n in chunks(wl, 8):
        grad = conv_chunk(buf, w, c0, n, True)
        for q in range(n):
            out[c0 + q] = grad[q, OFF : OFF + hl].astype(BF16)


def split_kernel(blocks, where, keep, came, own, *messages):
    iy, ix = where[0], where[1]
    ny = blocks // 2
    size = keep.shape[1] // blocks
    x = lax.rem(lax.div(ix, 2), 2)

    def block(y, b):
        at = pl.multiple_of((y * 2 + b) * size, size)
        return keep[:, pl.ds(at, size), :] + came[:, pl.ds(at, size), :].astype(F32)

    own[...] = block(iy, x)
    m = 0
    for d in range(ny):
        for b in range(2):
            if d or b:
                y = lax.rem(iy + d, ny)
                messages[m][...] = block(y, x if b == 0 else 1 - x).astype(BF16)
                m += 1


def reduce_filter(where, keep, send, nx, ny, iy, ix):
    other_core = [(i, i ^ 1) for i in range(nx)]
    came = lax.ppermute(send, "gx", other_core)
    blocks = 2 * ny
    taps, ch, half = keep.shape
    size = ch // blocks
    outs = [((taps, size, half), F32)] + [((taps, size, half), BF16)] * (blocks - 1)
    parts = call(functools.partial(split_kernel, blocks), outs, (where, keep, came))
    total, messages = parts[0], parts[1:]
    arrived = []
    m = 0
    for d in range(ny):
        for b in range(2):
            if d or b:
                pairs = [
                    (g * ny + y, (g ^ (2 * b)) * ny + (y + d) % ny) for g in range(nx) for y in range(ny)
                ]
                arrived.append(lax.ppermute(messages[m], ("gx", "gy"), pairs))
                m += 1
    for part in arrived:
        total = total + part.astype(F32)
    total = total.astype(BF16)
    bits = [1 << b for b in range(2, nx.bit_length() - 1)]
    for step in range(len(bits)):
        near, far = bits[step], bits[len(bits) - 1 - step]
        pairs = [(g, g ^ (near if g % 2 == 0 else far)) for g in range(nx)]
        part = lax.ppermute(total, "gx", pairs)
        total = (total.astype(F32) + part.astype(F32)).astype(BF16)
    beside = lax.ppermute(total, "gx", [(g, g ^ 2) for g in range(nx)])
    first = (ix // 2) % 2 == 0
    both = jnp.concatenate(
        [jnp.where(first, total, beside), jnp.where(first, beside, total)], axis=1
    )
    rest = lax.ppermute(both, "gx", other_core)
    low = ix % 2 == 0
    return jnp.concatenate([jnp.where(low, both, rest), jnp.where(low, rest, both)], axis=2)


def body(features, first_filter, second_filter, cotangent):
    ny, nx = lax.axis_size("gy"), lax.axis_size("gx")
    iy, ix = lax.axis_index("gy"), lax.axis_index("gx")
    hl, wl, ch = features.shape
    co = first_filter.shape[0]
    height, width = hl * ny, wl * nx
    rows = -(-(hl + 2 * OFF) // 16) * 16
    dims = (ny, hl, wl, height, width)
    scale_factor = 1.0 / math.sqrt(height * width)
    where = jnp.stack([iy, ix]).astype(jnp.int32)
    core = ix % 2
    forward = [(i, i + 1) for i in range(nx - 1)]
    backward = [(i + 1, i) for i in range(nx - 1)]

    def round_y(x, d):
        return lax.ppermute(x, "gy", [(i, (i + d) % ny) for i in range(ny)])

    def gathered(taps):
        half = co // 2
        send = lax.dynamic_slice_in_dim(taps, core * half, half, 1)
        mine = jnp.stack([round_y(send, d) for d in range(1, ny)])
        return mine, lax.ppermute(mine, "gx", [(i, i ^ 1) for i in range(nx)])

    first_own = jnp.transpose(first_filter, (2, 1, 0, 3)).reshape(9, co, ch)
    second_own = jnp.transpose(second_filter, (2, 1, 0, 3)).reshape(9, co, ch)
    first_in = gathered(first_own)
    second_in = gathered(second_own)

    ft = jnp.transpose(features, (1, 0, 2))
    left = lax.ppermute(ft[wl - 4 :], "gx", forward)
    right = lax.ppermute(ft[:4], "gx", backward)
    strip = jnp.concatenate([left, ft, right], axis=0)
    if ny == 2:
        up = down = round_y(jnp.where(iy == 0, strip[:, hl - OFF :], strip[:, :OFF]), 1)
    else:
        up = round_y(strip[:, hl - OFF :], 1)
        down = round_y(strip[:, :OFF], ny - 1)

    ct = jnp.transpose(cotangent, (1, 2, 0))
    ct = jnp.concatenate(
        [lax.ppermute(ct[wl - 2 :], "gx", forward), ct, lax.ppermute(ct[:2], "gx", backward)], axis=0
    )
    ct = jnp.pad(ct, ((0, 0), (OFF, rows - OFF - hl), (0, 0)))

    def rows_of(y):
        return lax.dynamic_slice_in_dim(ct, y * hl, rows, 1)

    cots = [rows_of(iy)] + [round_y(rows_of((iy + d) % ny), d) for d in range(1, ny)]
    if ny != 2:
        full = jnp.zeros((wl + 4, rows, ch), BF16)
        for d, part in enumerate(cots):
            full = lax.dynamic_update_slice_in_dim(full, part, ((iy - d) % ny) * co, 2)
        cots = [full]

    bf = lambda *s: pltpu.VMEM(s, BF16)
    weights = bf(9, ch, ch)
    tap_flops = 2 * 9 * ch * ch * rows

    fbuf_shape = ((wl + 8, rows, ch), BF16)
    hidden, slope1, fbuf = call(
        functools.partial(conv1_kernel, dims),
        [((wl + 6, rows, ch), BF16), ((wl + 2, rows, ch), F32), fbuf_shape],
        (where, ft, left, right, up, down, first_own, *first_in),
        [weights, bf(wl + 8, rows, 3 * ch)],
        tap_flops * (wl + 6),
    )
    act, slope2 = call(
        functools.partial(conv2_kernel, dims),
        [((wl, hl, ch), BF16), ((wl + 4, rows, ch), F32)],
        (where, hidden, second_own, *second_in),
        [weights, bf(wl + 6, rows, 3 * ch)],
        tap_flops * (wl + 4),
    )
    grad_shapes = [((9, ch, ch // 2), F32), ((9, ch, ch // 2), BF16)]
    outer, keep2, send2 = call(
        functools.partial(outer_kernel, dims, len(cots)),
        [((wl + 4, rows, ch), BF16)] + grad_shapes,
        (where, hidden, slope2, *cots),
        [bf(wl + 2, rows, 3 * ch), bf(ch, wl * rows)],
        tap_flops * wl,
    )
    inner, keep1, send1 = call(
        functools.partial(inner_kernel, dims),
        [((wl + 2, rows, ch), BF16)] + grad_shapes,
        (where, outer, second_own, *second_in, slope1, fbuf),
        [weights, bf(wl + 4, rows, 3 * ch), bf(ch, wl * rows)],
        tap_flops * (2 * wl + 2),
    )
    (input_grad,) = call(
        functools.partial(input_kernel, dims),
        [((wl, hl, ch), BF16)],
        (where, inner, first_own, *first_in),
        [weights, bf(wl + 2, rows, 3 * ch)],
        tap_flops * wl,
    )
    input_grad = jnp.transpose(input_grad, (1, 0, 2))

    def channels_of(y):
        return lax.dynamic_slice_in_dim(act, y * co, co, 2)

    parts = [channels_of(iy)] + [round_y(channels_of((iy + d) % ny), d) for d in range(1, ny)]
    output = jnp.zeros((wl, height, co), BF16)
    for d, part in enumerate(parts):
        output = lax.dynamic_update_slice_in_dim(output, part, ((iy - d) % ny) * hl, 1)
    output = jnp.transpose(output, (2, 0, 1))

    grads = []
    for keep, send in ((keep1, send1), (keep2, send2)):
        total = reduce_filter(where, keep, send, nx, ny, iy, ix)
        total = total.astype(F32) * scale_factor
        grads.append(jnp.transpose(total.reshape(3, 3, co, ch), (2, 1, 0, 3)))
    return output, input_grad, grads[0], grads[1]


def solution(mesh):
    in_specs = (
        P("gy", "gx", None),
        P("gy", None, None, None),
        P("gy", None, None, None),
        P("gy", "gx", None),
    )
    out_specs = (
        P("gy", "gx", None),
        P("gy", "gx", None),
        P("gy", None, None, None),
        P("gy", None, None, None),
    )
    return jax.shard_map(body, mesh=mesh, in_specs=in_specs, out_specs=out_specs, check_vma=False)
```

```python
import functools
import math

import jax
import jax.numpy as jnp
from jax import lax
from jax.experimental import pallas as pl
from jax.experimental.pallas import tpu as pltpu
from jax.sharding import PartitionSpec as P

F32, BF16 = jnp.float32, jnp.bfloat16
OFF = 8
HALO = 4
VMEM_LIMIT = 30 * 1024 * 1024
NT = (((1,), (1,)), ((), ()))
TN = (((0,), (0,)), ((), ()))


def call(kernel, outs, args, scratch=(), flops=0, smem_args=1):
    specs = [pl.BlockSpec(memory_space=pltpu.SMEM)] * smem_args
    specs += [pl.BlockSpec(memory_space=pltpu.VMEM)] * (len(args) - smem_args)
    nbytes = sum(a.size * a.dtype.itemsize for a in args[smem_args:])
    nbytes += sum(math.prod(s) * jnp.dtype(t).itemsize for s, t in outs)
    return pl.pallas_call(
        kernel,
        out_shape=[jax.ShapeDtypeStruct(s, t) for s, t in outs],
        in_specs=specs,
        out_specs=[pl.BlockSpec(memory_space=pltpu.VMEM)] * len(outs),
        scratch_shapes=list(scratch),
        compiler_params=pltpu.CompilerParams(vmem_limit_bytes=VMEM_LIMIT),
        cost_estimate=pl.CostEstimate(flops=flops, bytes_accessed=nbytes, transcendentals=0),
    )(*args)


def silu_parts(pre):
    sigma = 1.0 / (1.0 + jnp.exp(-pre))
    return pre * sigma, sigma * (1.0 + pre * (1.0 - sigma))


def row_mask(first, rows, total):
    at = lax.broadcasted_iota(jnp.int32, (rows, 1), 0) + (first - OFF)
    return (at >= 0) & (at < total)


def conv_chunk(x, w, c0, n, backward):
    rows, ch = x.shape[1], x.shape[2]
    sums = []
    for i in range(3):
        total = None
        for j in range(3):
            lhs = x[c0 + j : c0 + j + n].reshape(n * rows, ch)
            if backward:
                term = jnp.dot(lhs, w[(2 - i) * 3 + (2 - j)], preferred_element_type=F32)
            else:
                term = lax.dot_general(lhs, w[i * 3 + j], NT, preferred_element_type=F32)
            total = term if total is None else total + term
        sums.append(total.reshape(n, rows, ch))
    return [pltpu.roll(sums[0][q], 1, 0) + sums[1][q] + pltpu.roll(sums[2][q], rows - 1, 0) for q in range(n)]


def chunks(total, most):
    parts = -(-total // most)
    base, extra = divmod(total, parts)
    out, at = [], 0
    for p in range(parts):
        n = base + (p < extra)
        out.append((at, n))
        at += n
    return out


def assemble_filter(w, own, pieces, iy, core, ny):
    co = own.shape[1]
    half = co // 2
    w[:, pl.ds(pl.multiple_of(iy * co, co), co), :] = own[...]
    for d in range(1, ny):
        src = lax.rem(iy - d + ny, ny)
        mine, other = pieces
        at = pl.multiple_of(src * co + core * half, half)
        w[:, pl.ds(at, half), :] = mine[d - 1]
        at = pl.multiple_of(src * co + (1 - core) * half, half)
        w[:, pl.ds(at, half), :] = other[d - 1]


def conv1_kernel(dims, where, ft, left, right, up, down, own, mine, other, hidden, slope, fbuf, w):
    ny, hl, wl, height, width = dims
    iy, ix = where[0], where[1]
    rows, ch = fbuf.shape[1], fbuf.shape[2]
    ok = row_mask(iy * hl, rows, height)
    groups = ch // 128
    gap = jnp.zeros((rows - hl - OFF - HALO, ch), F32)
    for c in range(wl + 2 * HALO):
        if HALO <= c < wl + HALO:
            mid = ft[c - HALO].astype(F32)
        else:
            ref, at = (left, c) if c < HALO else (right, c - wl - HALO)
            mid = jnp.concatenate([ref[g * HALO + at].astype(F32) for g in range(groups)], axis=1)
        r = (c % 2) * HALO
        above = up[c // 2].astype(F32)[r : r + HALO]
        below = down[c // 2].astype(F32)[r : r + HALO]
        x = jnp.concatenate([gap[: OFF - HALO], above, mid, below, gap], axis=0)
        fbuf[c] = jnp.where(ok, x, 0.0).astype(BF16)
    assemble_filter(w, own, (mine, other), iy, ix % 2, ny)
    for c0, n in chunks(wl + 6, 11):
        pre = conv_chunk(fbuf, w, c0, n, False)
        for q in range(n):
            c = c0 + q
            col = ix * wl + c - 3
            act, grad = silu_parts(pre[q])
            inside = ok & (col >= 0) & (col < width)
            hidden[c] = jnp.where(inside, act, 0.0).astype(BF16)
            if 2 <= c < wl + 4:
                slope[c - 2] = jnp.where(inside, grad, 0.0)


def conv2_kernel(dims, where, hidden, own, mine, other, act_out, slope, w):
    ny, hl, wl, height, width = dims
    iy, ix = where[0], where[1]
    rows = hidden.shape[1]
    ok = row_mask(iy * hl, rows, height)
    assemble_filter(w, own, (mine, other), iy, ix % 2, ny)
    for c0, n in chunks(wl + 4, 10):
        pre = conv_chunk(hidden, w, c0, n, False)
        for q in range(n):
            c = c0 + q
            col = ix * wl + c - 2
            act, grad = silu_parts(pre[q])
            inside = ok & (col >= 0) & (col < width)
            slope[c] = jnp.where(inside, grad, 0.0)
            if 2 <= c < wl + 2:
                act_out[c - 2] = act[OFF : OFF + hl].astype(BF16)


def own_rows(rows, hl):
    at = lax.broadcasted_iota(jnp.int32, (rows, 1), 0)
    return (at >= OFF) & (at < OFF + hl)


def put_shifted(shifted, c, grad, own):
    rows, ch = grad.shape
    grad = jnp.where(own, grad, 0.0)
    for i in range(3):
        part = grad if i == 1 else pltpu.roll(grad, (i - 1) % rows, 0)
        shifted[c * rows : (c + 1) * rows, i * ch : (i + 1) * ch] = part.astype(BF16)


def filter_grad(where, x, first, shifted, wl, keep, send):
    low_core = where[1] % 2 == 0
    rows, ch = x.shape[1], x.shape[2]
    half = ch // 2
    for j in range(3):
        rhs = x[first + j : first + j + wl].reshape(wl * rows, ch)
        g = lax.dot_general(shifted[...], rhs, TN, preferred_element_type=F32)
        for i in range(3):
            low, high = g[i * ch : (i + 1) * ch, :half], g[i * ch : (i + 1) * ch, half:]
            keep[i * 3 + j] = jnp.where(low_core, low, high)
            send[i * 3 + j] = jnp.where(low_core, high, low).astype(BF16)


def outer_kernel(dims, count, where, hidden, slope, *refs):
    cots, (outer, keep, send, shifted) = refs[:count], refs[count:]
    ny, hl, wl, height, width = dims
    iy = where[0]
    rows = hidden.shape[1]
    own = own_rows(rows, hl)
    for c in range(wl + 4):
        parts = [ref[c].astype(F32) for ref in cots]
        if len(parts) == 2:
            a, b = parts
            parts = [jnp.where(iy == 0, a, b), jnp.where(iy == 0, b, a)]
        val = (jnp.concatenate(parts, axis=1) * slope[c]).astype(BF16)
        outer[c] = val
        if 2 <= c < wl + 2:
            put_shifted(shifted, c - 2, val.astype(F32), own)
    filter_grad(where, hidden, 2, shifted, wl, keep, send)


def inner_kernel(dims, where, outer, own, mine, other, slope, fbuf, inner, keep, send, w, shifted):
    ny, hl, wl, height, width = dims
    iy, ix = where[0], where[1]
    rows = fbuf.shape[1]
    assemble_filter(w, own, (mine, other), iy, ix % 2, ny)
    mine_rows = own_rows(rows, hl)
    for c0, n in chunks(wl + 2, 9):
        grad = conv_chunk(outer, w, c0, n, True)
        for q in range(n):
            c = c0 + q
            val = (grad[q] * slope[c]).astype(BF16)
            inner[c] = val
            if 1 <= c < wl + 1:
                put_shifted(shifted, c - 1, val.astype(F32), mine_rows)
    filter_grad(where, fbuf, 3, shifted, wl, keep, send)


def input_kernel(dims, where, inner, own, mine, other, out, w):
    ny, hl, wl, height, width = dims
    iy, ix = where[0], where[1]
    assemble_filter(w, own, (mine, other), iy, ix % 2, ny)
    for c0, n in chunks(wl, 8):
        grad = conv_chunk(inner, w, c0, n, True)
        for q in range(n):
            out[c0 + q] = grad[q][OFF : OFF + hl].astype(BF16)


def split_kernel(blocks, where, keep, came, own, *messages):
    iy, ix = where[0], where[1]
    ny = blocks // 2
    size = keep.shape[1] // blocks
    x = lax.rem(lax.div(ix, 2), 2)

    def block(y, b):
        at = pl.multiple_of((y * 2 + b) * size, size)
        return keep[:, pl.ds(at, size), :] + came[:, pl.ds(at, size), :].astype(F32)

    own[...] = block(iy, x)
    m = 0
    for d in range(ny):
        for b in range(2):
            if d or b:
                y = lax.rem(iy + d, ny)
                messages[m][...] = block(y, x if b == 0 else 1 - x).astype(BF16)
                m += 1


def reduce_filter(where, keep, send, nx, ny, iy, ix):
    other_core = [(i, i ^ 1) for i in range(nx)]
    came = lax.ppermute(send, "gx", other_core)
    blocks = 2 * ny
    taps, ch, half = keep.shape
    size = ch // blocks
    outs = [((taps, size, half), F32)] + [((taps, size, half), BF16)] * (blocks - 1)
    parts = call(functools.partial(split_kernel, blocks), outs, (where, keep, came))
    total, messages = parts[0], parts[1:]
    arrived = []
    m = 0
    for d in range(ny):
        for b in range(2):
            if d or b:
                pairs = [
                    (g * ny + y, (g ^ (2 * b)) * ny + (y + d) % ny) for g in range(nx) for y in range(ny)
                ]
                arrived.append(lax.ppermute(messages[m], ("gx", "gy"), pairs))
                m += 1
    for part in arrived:
        total = total + part.astype(F32)
    total = total.astype(BF16)
    bits = [1 << b for b in range(2, nx.bit_length() - 1)]
    for step in range(len(bits)):
        near, far = bits[step], bits[len(bits) - 1 - step]
        pairs = [(g, g ^ (near if g % 2 == 0 else far)) for g in range(nx)]
        part = lax.ppermute(total, "gx", pairs)
        total = (total.astype(F32) + part.astype(F32)).astype(BF16)
    beside = lax.ppermute(total, "gx", [(g, g ^ 2) for g in range(nx)])
    first = (ix // 2) % 2 == 0
    both = jnp.concatenate(
        [jnp.where(first, total, beside), jnp.where(first, beside, total)], axis=1
    )
    rest = lax.ppermute(both, "gx", other_core)
    low = ix % 2 == 0
    return jnp.concatenate([jnp.where(low, both, rest), jnp.where(low, rest, both)], axis=2)


def body(features, first_filter, second_filter, cotangent):
    ny, nx = lax.axis_size("gy"), lax.axis_size("gx")
    iy, ix = lax.axis_index("gy"), lax.axis_index("gx")
    hl, wl, ch = features.shape
    co = first_filter.shape[0]
    height, width = hl * ny, wl * nx
    rows = -(-(hl + 2 * OFF) // 16) * 16
    dims = (ny, hl, wl, height, width)
    scale_factor = 1.0 / math.sqrt(height * width)
    where = jnp.stack([iy, ix]).astype(jnp.int32)
    core = ix % 2
    forward = [(i, i + 1) for i in range(nx - 1)]
    backward = [(i + 1, i) for i in range(nx - 1)]

    def round_y(x, d):
        return lax.ppermute(x, "gy", [(i, (i + d) % ny) for i in range(ny)])

    def gathered(taps):
        half = co // 2
        send = lax.dynamic_slice_in_dim(taps, core * half, half, 1)
        mine = jnp.stack([round_y(send, d) for d in range(1, ny)])
        return mine, lax.ppermute(mine, "gx", [(i, i ^ 1) for i in range(nx)])

    def halves(taps):
        return lax.dynamic_slice_in_dim(taps, core * (co // 2), co // 2, 1)

    def spread(send):
        mine = jnp.stack([round_y(send, d) for d in range(1, ny)])
        return mine, lax.ppermute(mine, "gx", [(i, i ^ 1) for i in range(nx)])

    first_own = jnp.transpose(first_filter, (1, 2, 0, 3)).reshape(9, co, ch)
    second_own = jnp.transpose(second_filter, (1, 2, 0, 3)).reshape(9, co, ch)
    first_send = halves(first_own)
    first_send, features, cotangent = lax.optimization_barrier((first_send, features, cotangent))
    first_in = spread(first_send)

    ft = jnp.transpose(features, (1, 0, 2))
    ct = jnp.transpose(cotangent, (1, 2, 0))
    groups = ch // 128

    def edge(f, c):
        planes = [f[:, :, g * 128 : (g + 1) * 128] for g in range(groups)]
        return jnp.concatenate(planes + [c.reshape(2 * groups, hl, 128)], axis=0)

    left = lax.ppermute(edge(ft[wl - HALO :], ct[wl - 2 :]), "gx", forward)
    right = lax.ppermute(edge(ft[:HALO], ct[:2]), "gx", backward)

    def edge_rows(h0):
        def of(planes):
            return jnp.concatenate([planes[g * HALO : (g + 1) * HALO, h0 : h0 + HALO] for g in range(groups)], axis=2)

        strip = jnp.concatenate([of(left), ft[:, h0 : h0 + HALO], of(right)], axis=0)
        return strip.reshape(wl // 2 + HALO, 2 * HALO, ch)

    if ny == 2:
        row_send = jnp.where(iy == 0, edge_rows(hl - HALO), edge_rows(0))
        second_own, row_send = lax.optimization_barrier((second_own, row_send))
        up = down = round_y(row_send, 1)
    else:
        up = round_y(edge_rows(hl - HALO), 1)
        down = round_y(edge_rows(0), ny - 1)
    second_in = spread(halves(second_own))

    at = groups * HALO
    ct = jnp.concatenate(
        [left[at:].reshape(2, height, co), ct, right[at:].reshape(2, height, co)], axis=0
    )
    ct = jnp.pad(ct, ((0, 0), (OFF, rows - OFF - hl), (0, 0)))

    def rows_of(y):
        return lax.dynamic_slice_in_dim(ct, y * hl, rows, 1)

    cot_send = [rows_of((iy + d) % ny) for d in range(1, ny)]
    (cot_send, first_in) = lax.optimization_barrier((cot_send, first_in))
    cots = [rows_of(iy)] + [round_y(cot_send[d - 1], d) for d in range(1, ny)]
    if ny != 2:
        full = jnp.zeros((wl + 4, rows, ch), BF16)
        for d, part in enumerate(cots):
            full = lax.dynamic_update_slice_in_dim(full, part, ((iy - d) % ny) * co, 2)
        cots = [full]

    bf = lambda *s: pltpu.VMEM(s, BF16)
    weights = bf(9, ch, ch)
    tap_flops = 2 * 9 * ch * ch * rows

    fbuf_shape = ((wl + 8, rows, ch), BF16)
    hidden, slope1, fbuf = call(
        functools.partial(conv1_kernel, dims),
        [((wl + 6, rows, ch), BF16), ((wl + 2, rows, ch), F32), fbuf_shape],
        (where, ft, left, right, up, down, first_own, *first_in),
        [weights],
        tap_flops * (wl + 6),
    )
    act, slope2 = call(
        functools.partial(conv2_kernel, dims),
        [((wl, hl, ch), BF16), ((wl + 4, rows, ch), F32)],
        (where, hidden, second_own, *second_in),
        [weights],
        tap_flops * (wl + 4),
    )
    grad_shapes = [((9, ch, ch // 2), F32), ((9, ch, ch // 2), BF16)]
    outer, keep2, send2 = call(
        functools.partial(outer_kernel, dims, len(cots)),
        [((wl + 4, rows, ch), BF16)] + grad_shapes,
        (where, hidden, slope2, *cots),
        [bf(wl * rows, 3 * ch)],
        tap_flops * wl,
    )
    inner, keep1, send1 = call(
        functools.partial(inner_kernel, dims),
        [((wl + 2, rows, ch), BF16)] + grad_shapes,
        (where, outer, second_own, *second_in, slope1, fbuf),
        [weights, bf(wl * rows, 3 * ch)],
        tap_flops * (2 * wl + 2),
    )
    (input_grad,) = call(
        functools.partial(input_kernel, dims),
        [((wl, hl, ch), BF16)],
        (where, inner, first_own, *first_in),
        [weights],
        tap_flops * wl,
    )
    input_grad = jnp.transpose(input_grad, (1, 0, 2))

    def channels_of(y):
        return lax.dynamic_slice_in_dim(act, y * co, co, 2)

    parts = [channels_of(iy)] + [round_y(channels_of((iy + d) % ny), d) for d in range(1, ny)]
    output = jnp.zeros((wl, height, co), BF16)
    for d, part in enumerate(parts):
        output = lax.dynamic_update_slice_in_dim(output, part, ((iy - d) % ny) * hl, 1)
    output = jnp.transpose(output, (2, 0, 1))

    grads = []
    for keep, send in ((keep1, send1), (keep2, send2)):
        total = reduce_filter(where, keep, send, nx, ny, iy, ix)
        total = total.astype(F32) * scale_factor
        grads.append(jnp.transpose(total.reshape(3, 3, co, ch), (2, 0, 1, 3)))
    return output, input_grad, grads[0], grads[1]


def solution(mesh):
    in_specs = (
        P("gy", "gx", None),
        P("gy", None, None, None),
        P("gy", None, None, None),
        P("gy", "gx", None),
    )
    out_specs = (
        P("gy", "gx", None),
        P("gy", "gx", None),
        P("gy", None, None, None),
        P("gy", None, None, None),
    )
    return jax.shard_map(body, mesh=mesh, in_specs=in_specs, out_specs=out_specs, check_vma=False)
```

```python
import functools
import math

import jax
import jax.numpy as jnp
from jax import lax
from jax.experimental import pallas as pl
from jax.experimental.pallas import tpu as pltpu
from jax.sharding import PartitionSpec as P

F32, BF16 = jnp.float32, jnp.bfloat16
OFF = 8
HALO = 4
VMEM_LIMIT = 30 * 1024 * 1024
NT = (((1,), (1,)), ((), ()))
TN = (((0,), (0,)), ((), ()))


def call(kernel, outs, args, scratch=(), flops=0, smem_args=1):
    specs = [pl.BlockSpec(memory_space=pltpu.SMEM)] * smem_args
    specs += [pl.BlockSpec(memory_space=pltpu.VMEM)] * (len(args) - smem_args)


    return pl.pallas_call(
        kernel,
        out_shape=[jax.ShapeDtypeStruct(s, t) for s, t in outs],
        in_specs=specs,
        out_specs=[pl.BlockSpec(memory_space=pltpu.VMEM)] * len(outs),
        scratch_shapes=list(scratch),
        compiler_params=pltpu.CompilerParams(vmem_limit_bytes=VMEM_LIMIT),
        cost_estimate=pl.CostEstimate(flops=0, bytes_accessed=0, transcendentals=0),
    )(*args)


def silu_parts(pre):
    sigma = 1.0 / (1.0 + jnp.exp(-pre))
    return pre * sigma, sigma * (1.0 + pre * (1.0 - sigma))


def after(x, *others):
    return lax.optimization_barrier((x, others))[0]


def row_mask(first, rows, total):
    at = lax.broadcasted_iota(jnp.int32, (rows, 1), 0) + (first - OFF)
    return (at >= 0) & (at < total)


def conv_chunk(x, w, c0, n, backward):
    rows, ch = x.shape[1], x.shape[2]
    sums = []
    for i in range(3):
        total = None
        for j in range(3):
            lhs = x[c0 + j : c0 + j + n].reshape(n * rows, ch)
            if backward:
                term = jnp.dot(lhs, w[(2 - i) * 3 + (2 - j)], preferred_element_type=F32)
            else:
                term = lax.dot_general(lhs, w[i * 3 + j], NT, preferred_element_type=F32)
            total = term if total is None else total + term
        sums.append(total.reshape(n, rows, ch))
    return [pltpu.roll(sums[0][q], 1, 0) + sums[1][q] + pltpu.roll(sums[2][q], rows - 1, 0) for q in range(n)]


def chunks(total, most):
    parts = -(-total // most)
    base, extra = divmod(total, parts)
    out, at = [], 0
    for p in range(parts):
        n = base + (p < extra)
        out.append((at, n))
        at += n
    return out


def assemble_filter(w, own, pieces, iy, core, ny):
    co = own.shape[1]
    half = co // 2
    w[:, pl.ds(pl.multiple_of(iy * co, co), co), :] = own[...]
    for d in range(1, ny):
        src = lax.rem(iy - d + ny, ny)
        mine, other = pieces
        at = pl.multiple_of(src * co + core * half, half)
        w[:, pl.ds(at, half), :] = mine[d - 1]
        at = pl.multiple_of(src * co + (1 - core) * half, half)
        w[:, pl.ds(at, half), :] = other[d - 1]


def conv1_kernel(dims, where, ft, left, right, up, down, own, mine, other, hidden, slope, fbuf, w):
    ny, hl, wl, height, width = dims
    iy, ix = where[0], where[1]
    rows, ch = fbuf.shape[1], fbuf.shape[2]
    ok = row_mask(iy * hl, rows, height)
    groups, tall = ch // 128, hl + 2 * HALO
    before = jnp.zeros((OFF - HALO, ch), F32)
    after = jnp.zeros((rows - hl - OFF - HALO, ch), F32)
    for c in range(wl + 2 * HALO):
        if HALO <= c < wl + HALO:
            q = c - HALO
            mid = [up[q].astype(F32), ft[q].astype(F32), down[q].astype(F32)]
        else:
            ref, q = (left, c) if c < HALO else (right, c - wl - HALO)
            planes = [ref[(g * HALO + q) * tall : (g * HALO + q + 1) * tall].astype(F32) for g in range(groups)]
            mid = [jnp.concatenate(planes, axis=1)]
        x = jnp.concatenate([before] + mid + [after], axis=0)
        fbuf[c] = jnp.where(ok, x, 0.0).astype(BF16)
    assemble_filter(w, own, (mine, other), iy, ix % 2, ny)
    for c0, n in chunks(wl + 6, 11):
        pre = conv_chunk(fbuf, w, c0, n, False)
        for q in range(n):
            c = c0 + q
            col = ix * wl + c - 3
            act, grad = silu_parts(pre[q])
            inside = ok & (col >= 0) & (col < width)
            hidden[c] = jnp.where(inside, act, 0.0).astype(BF16)
            if 2 <= c < wl + 4:
                slope[c - 2] = jnp.where(inside, grad, 0.0)


def conv2_kernel(dims, where, hidden, own, mine, other, act_out, slope, w):
    ny, hl, wl, height, width = dims
    iy, ix = where[0], where[1]
    rows = hidden.shape[1]
    ok = row_mask(iy * hl, rows, height)
    assemble_filter(w, own, (mine, other), iy, ix % 2, ny)
    for c0, n in chunks(wl + 4, 10):
        pre = conv_chunk(hidden, w, c0, n, False)
        for q in range(n):
            c = c0 + q
            col = ix * wl + c - 2
            act, grad = silu_parts(pre[q])
            inside = ok & (col >= 0) & (col < width)
            slope[c] = jnp.where(inside, grad, 0.0)
            if 2 <= c < wl + 2:
                act_out[c - 2] = act[OFF : OFF + hl].astype(BF16)


def edge_kernel(dims, where, ft, up, down, ct_low, ct_high, low, high):
    ny, hl, wl, height, width = dims
    ch = ft.shape[2]
    groups, tall = ch // 128, hl + 2 * HALO
    for out, first, cot in ((low, 0, ct_low), (high, wl - HALO, ct_high)):
        for q in range(HALO):
            c = first + q
            x = jnp.concatenate([up[c].astype(F32), ft[c].astype(F32), down[c].astype(F32)], axis=0).astype(BF16)
            for g in range(groups):
                at = (g * HALO + q) * tall
                out[at : at + tall] = x[:, g * 128 : (g + 1) * 128]
        out[groups * HALO * tall :] = cot[...]


def own_rows(rows, hl):
    at = lax.broadcasted_iota(jnp.int32, (rows, 1), 0)
    return (at >= OFF) & (at < OFF + hl)


def put_shifted(shifted, c, grad, own):
    rows, ch = grad.shape
    grad = jnp.where(own, grad, 0.0)
    for i in range(3):
        part = grad if i == 1 else pltpu.roll(grad, (i - 1) % rows, 0)
        shifted[c * rows : (c + 1) * rows, i * ch : (i + 1) * ch] = part.astype(BF16)


def filter_grad(where, x, first, shifted, wl, keep, send):
    low_core = where[1] % 2 == 0
    rows, ch = x.shape[1], x.shape[2]
    half = ch // 2
    for j in range(3):
        rhs = x[first + j : first + j + wl].reshape(wl * rows, ch)
        g = lax.dot_general(shifted[...], rhs, TN, preferred_element_type=F32)
        for i in range(3):
            low, high = g[i * ch : (i + 1) * ch, :half], g[i * ch : (i + 1) * ch, half:]
            keep[i * 3 + j] = jnp.where(low_core, low, high)
            send[i * 3 + j] = jnp.where(low_core, high, low).astype(BF16)


def inner_kernel(dims, count, where, own, mine, other, slope2, slope1, fbuf, *refs):
    cots, (inner, outer, keep, send, w, shifted) = refs[:count], refs[count:]
    ny, hl, wl, height, width = dims
    iy, ix = where[0], where[1]
    rows = fbuf.shape[1]
    mine_rows = own_rows(rows, hl)
    for c in range(wl + 4):
        parts = [ref[c].astype(F32) for ref in cots]
        if len(parts) == 2:
            gap = jnp.zeros((OFF, parts[0].shape[1]), F32)
            a, b = [
                jnp.where(iy == 0, jnp.concatenate([gap, p], axis=0), jnp.concatenate([p, gap], axis=0))
                for p in parts
            ]
            parts = [jnp.where(iy == 0, a, b), jnp.where(iy == 0, b, a)]
        outer[c] = (jnp.concatenate(parts, axis=1) * slope2[c]).astype(BF16)
    assemble_filter(w, own, (mine, other), iy, ix % 2, ny)
    for c0, n in chunks(wl + 2, 9):
        grad = conv_chunk(outer, w, c0, n, True)
        for q in range(n):
            c = c0 + q
            val = (grad[q] * slope1[c]).astype(BF16)
            inner[c] = val
            if 1 <= c < wl + 1:
                put_shifted(shifted, c - 1, val.astype(F32), mine_rows)
    filter_grad(where, fbuf, 3, shifted, wl, keep, send)


def second_grad_kernel(dims, where, hidden, outer, keep, send, shifted):
    ny, hl, wl, height, width = dims
    own = own_rows(hidden.shape[1], hl)
    for c in range(wl):
        put_shifted(shifted, c, outer[c + 2].astype(F32), own)
    filter_grad(where, hidden, 2, shifted, wl, keep, send)


def input_kernel(dims, where, inner, own, mine, other, out, w, flat):
    ny, hl, wl, height, width = dims
    iy, ix = where[0], where[1]
    assemble_filter(w, own, (mine, other), iy, ix % 2, ny)
    for c0, n in chunks(wl, 8):
        grad = conv_chunk(inner, w, c0, n, True)
        for q in range(n):
            for g in range(flat.shape[0]):
                part = grad[q][OFF : OFF + hl, g * 128 : (g + 1) * 128]
                flat[g, pl.ds(c0 + q, hl, stride=wl), :] = part
    for g in range(flat.shape[0]):
        out[:, :, g * 128 : (g + 1) * 128] = flat[g].reshape(hl, wl, 128).astype(BF16)


def split_kernel(blocks, where, keep, came, own, *messages):
    iy, ix = where[0], where[1]
    ny = blocks // 2
    size = keep.shape[1] // blocks
    x = lax.rem(lax.div(ix, 2), 2)

    def block(y, b):
        at = pl.multiple_of((y * 2 + b) * size, size)
        return keep[:, pl.ds(at, size), :] + came[:, pl.ds(at, size), :].astype(F32)

    own[...] = block(iy, x)
    m = 0
    for d in range(ny):
        for b in range(2):
            if d or b:
                y = lax.rem(iy + d, ny)
                messages[m][...] = block(y, x if b == 0 else 1 - x).astype(BF16)
                m += 1


def finish_kernel(scale, where, here, there, out):
    low_core = where[1] % 2 == 0
    for t in range(here.shape[0]):
        a, b = here[t].astype(F32) * scale, there[t].astype(F32) * scale
        half = a.shape[1]
        out[t, :, :half] = jnp.where(low_core, a, b)
        out[t, :, half:] = jnp.where(low_core, b, a)


def halving_kernel(where, keep, came, own, other, send):
    iy, ix = where[0], where[1]
    size = own.shape[1]
    x = lax.rem(lax.div(ix, 2), 2)
    by_y = lax.rem(ix, 2) == 0

    def block(y, b):
        at = pl.multiple_of((y * 2 + b) * size, size)
        return keep[:, pl.ds(at, size), :] + came[:, pl.ds(at, size), :].astype(F32)

    own[...] = block(iy, x)
    other[...] = block(jnp.where(by_y, iy, 1 - iy), jnp.where(by_y, 1 - x, x))
    send[0] = block(jnp.where(by_y, 1 - iy, iy), jnp.where(by_y, x, 1 - x)).astype(BF16)
    send[1] = block(1 - iy, 1 - x).astype(BF16)


def split_filter(where, keep, send, nx, ny):
    came = lax.ppermute(send, "gx", [(i, i ^ 1) for i in range(nx)])
    blocks = 2 * ny
    taps, ch, half = keep.shape
    shape = (taps, ch // blocks, half)
    if ny == 2:
        outs = [(shape, F32), (shape, F32), ((2,) + shape, BF16)]
        return call(halving_kernel, outs, (where, keep, came))
    outs = [(shape, F32)] + [(shape, BF16)] * (blocks - 1)
    return call(functools.partial(split_kernel, blocks), outs, (where, keep, came))


def send_planes(parts, nx, ny):
    arrived = []
    for d in range(ny):
        for b in range(2):
            if d or b:
                pairs = [
                    (g * ny + y, (g ^ (2 * b)) * ny + (y + d) % ny) for g in range(nx) for y in range(ny)
                ]
                arrived.append(lax.ppermute(parts[len(arrived) + 1], ("gx", "gy"), pairs))
    return arrived


def halving_pairs(nx, step):
    return [(g * 2 + y, g * 2 + 1 - y if g % 2 == step else (g ^ 2) * 2 + y) for g in range(nx) for y in range(2)]


def add(parts):
    total = parts[0].astype(F32)
    for part in parts[1:]:
        total = total + part.astype(F32)
    return total.astype(BF16)


def far_bits(nx):
    return [1 << b for b in range(2, nx.bit_length() - 1)]


def far_partner(total, step, nx):
    bits = far_bits(nx)
    near, far = bits[step], bits[len(bits) - 1 - step]
    return lax.ppermute(total, "gx", [(g, g ^ (near if g % 2 == 0 else far)) for g in range(nx)])


def finish(where, total, beside, nx, ix, scale):
    first = (ix // 2) % 2 == 0
    here = jnp.concatenate([jnp.where(first, total, beside), jnp.where(first, beside, total)], axis=1)
    there = lax.ppermute(here, "gx", [(g, g ^ 1) for g in range(nx)])
    taps, size, half = here.shape
    (out,) = call(functools.partial(finish_kernel, scale), [((taps, size, 2 * half), F32)], (where, here, there))
    return jnp.transpose(out.reshape(3, 3, size, 2 * half), (2, 0, 1, 3))


def body(features, first_filter, second_filter, cotangent):
    ny, nx = lax.axis_size("gy"), lax.axis_size("gx")
    iy, ix = lax.axis_index("gy"), lax.axis_index("gx")
    hl, wl, ch = features.shape
    co = first_filter.shape[0]
    height, width = hl * ny, wl * nx
    rows = -(-(hl + 2 * OFF) // 16) * 16
    dims = (ny, hl, wl, height, width)
    scale_factor = 1.0 / math.sqrt(height * width)
    where = jnp.stack([iy, ix]).astype(jnp.int32)
    core = ix % 2
    forward = [(i, i + 1) for i in range(nx - 1)]
    backward = [(i + 1, i) for i in range(nx - 1)]

    def round_y(x, d):
        return lax.ppermute(x, "gy", [(i, (i + d) % ny) for i in range(ny)])

    def gathered(taps):
        half = co // 2
        send = lax.dynamic_slice_in_dim(taps, core * half, half, 1)
        mine = jnp.stack([round_y(send, d) for d in range(1, ny)])
        return mine, lax.ppermute(mine, "gx", [(i, i ^ 1) for i in range(nx)])

    def halves(taps):
        return lax.dynamic_slice_in_dim(taps, core * (co // 2), co // 2, 1)

    def spread_y(send):
        return jnp.stack([round_y(send, d) for d in range(1, ny)])

    def pass_core(mine):
        return lax.ppermute(mine, "gx", [(i, i ^ 1) for i in range(nx)])

    if ny == 2:
        row_send = lax.dynamic_slice_in_dim(features, jnp.where(iy == 0, hl - HALO, 0), HALO, 0)
        up = down = jnp.transpose(round_y(row_send, 1), (1, 0, 2))
    else:
        row_send = (features[hl - HALO :], features[:HALO])
        up = jnp.transpose(round_y(row_send[0], 1), (1, 0, 2))
        down = jnp.transpose(round_y(row_send[1], ny - 1), (1, 0, 2))

    first_own = jnp.transpose(first_filter, (1, 2, 0, 3)).reshape(9, co, ch)
    second_own = jnp.transpose(second_filter, (1, 2, 0, 3)).reshape(9, co, ch)
    first_mine = spread_y(halves(after(first_own, row_send)))

    ft = jnp.transpose(after(features, row_send), (1, 0, 2))
    ct = jnp.transpose(cotangent, (1, 2, 0))
    groups, tall = ch // 128, hl + 2 * HALO
    at = groups * HALO * tall
    shape = ((at + 2 * height * co // 128, 128), BF16)
    low, high = call(
        functools.partial(edge_kernel, dims),
        [shape] * 2,
        (where, ft, up, down, ct[:2].reshape(-1, 128), ct[wl - 2 :].reshape(-1, 128)),
    )
    left = lax.ppermute(high, "gx", forward)
    right = lax.ppermute(low, "gx", backward)
    first_mine = after(first_mine, left, right)
    first_in = (first_mine, pass_core(first_mine))
    second_mine = spread_y(halves(after(second_own, up)))

    ct = jnp.concatenate([left[at:].reshape(2, height, co), ct, right[at:].reshape(2, height, co)], axis=0)
    if ny == 2:
        window = hl + OFF
        rows_of = lambda y: lax.dynamic_slice_in_dim(ct, y * (height - window), window, 1)
    else:
        ct = jnp.pad(ct, ((0, 0), (OFF, rows - OFF - hl), (0, 0)))
        rows_of = lambda y: lax.dynamic_slice_in_dim(ct, y * hl, rows, 1)
    cot_send = [rows_of((iy + d) % ny) for d in range(1, ny)]
    ft = after(ft, cot_send, second_mine)
    cots = [rows_of(iy)] + [round_y(cot_send[d - 1], d) for d in range(1, ny)]
    if ny != 2:
        full = jnp.zeros((wl + 4, rows, ch), BF16)
        for d, part in enumerate(cots):
            full = lax.dynamic_update_slice_in_dim(full, part, ((iy - d) % ny) * co, 2)
        cots = [full]

    bf = lambda *s: pltpu.VMEM(s, BF16)
    weights = bf(9, ch, ch)
    tap_flops = 2 * 9 * ch * ch * rows

    fbuf_shape = ((wl + 8, rows, ch), BF16)
    hidden, slope1, fbuf = call(
        functools.partial(conv1_kernel, dims),
        [((wl + 6, rows, ch), BF16), ((wl + 2, rows, ch), F32), fbuf_shape],
        (where, ft, left, right, up, down, first_own, *first_in),
        [weights],
        tap_flops * (wl + 6),
    )
    second_in = (second_mine, pass_core(second_mine))
    act, slope2 = call(
        functools.partial(conv2_kernel, dims),
        [((wl, hl, ch), BF16), ((wl + 4, rows, ch), F32)],
        (where, hidden, second_own, *second_in),
        [weights],
        tap_flops * (wl + 4),
    )
    grad_shapes = [((9, ch, ch // 2), F32), ((9, ch, ch // 2), BF16)]
    shifted = bf(wl * rows, 3 * ch)
    inner, outer, keep1, send1 = call(
        functools.partial(inner_kernel, dims, len(cots)),
        [((wl + 2, rows, ch), BF16), ((wl + 4, rows, ch), BF16)] + grad_shapes,
        (where, second_own, *second_in, slope2, slope1, fbuf, *cots),
        [weights, shifted],
        tap_flops * (2 * wl + 2),
    )
    keep2, send2 = call(
        functools.partial(second_grad_kernel, dims),
        grad_shapes,
        (where, hidden, outer),
        [shifted],
        tap_flops * wl,
    )
    parts1 = split_filter(where, keep1, send1, nx, ny)
    keep2 = after(keep2, parts1)
    parts2 = split_filter(where, keep2, send2, nx, ny)
    (input_grad,) = call(
        functools.partial(input_kernel, dims),
        [((hl, wl, ch), BF16)],
        (where, inner, first_own, *first_in),
        [weights, pltpu.VMEM((ch // 128, hl * wl, 128), F32)],
        tap_flops * wl,
    )
    if ny == 2:
        (own1, other1, send1), (own2, other2, send2) = parts1, parts2
        axes, pairs = ("gx", "gy"), [halving_pairs(nx, step) for step in range(2)]
        came1 = lax.ppermute(send1, axes, pairs[0])
        came2 = lax.ppermute(send2, axes, pairs[0])
        came1 = after(came1, parts2, input_grad)
        total1 = add([own1, came1[0], lax.ppermute(add([other1, came1[1]]), axes, pairs[1])])
        total2 = add([own2, came2[0], lax.ppermute(add([other2, came2[1]]), axes, pairs[1])])
    else:
        total1 = add([after(parts1[0], parts2, input_grad)] + send_planes(parts1, nx, ny))
        total2 = add([parts2[0]] + send_planes(parts2, nx, ny))
    act = after(act, total2)

    def channels_of(y):
        return lax.dynamic_slice_in_dim(act, y * co, co, 2)

    parts = [channels_of(iy)] + [round_y(channels_of((iy + d) % ny), d) for d in range(1, ny)]
    output = jnp.zeros((wl, height, co), BF16)
    for d, part in enumerate(parts):
        output = lax.dynamic_update_slice_in_dim(output, part, ((iy - d) % ny) * hl, 1)
    output = jnp.transpose(output, (2, 0, 1))

    for step in range(len(far_bits(nx))):
        other1 = far_partner(total1, step, nx)
        other2 = far_partner(total2, step, nx)
        total1 = add([total1, other1])
        total2 = add([total2, other2])
    total2 = after(total2, output)
    beside1 = lax.ppermute(total1, "gx", [(g, g ^ 2) for g in range(nx)])
    beside2 = lax.ppermute(total2, "gx", [(g, g ^ 2) for g in range(nx)])
    first_grad = finish(where, total1, beside1, nx, ix, scale_factor)
    second_grad = finish(where, total2, after(beside2, first_grad), nx, ix, scale_factor)
    return output, input_grad, first_grad, second_grad


def solution(mesh):
    in_specs = (
        P("gy", "gx", None),
        P("gy", None, None, None),
        P("gy", None, None, None),
        P("gy", "gx", None),
    )
    out_specs = (
        P("gy", "gx", None),
        P("gy", "gx", None),
        P("gy", None, None, None),
        P("gy", None, None, None),
    )
    return jax.shard_map(body, mesh=mesh, in_specs=in_specs, out_specs=out_specs, check_vma=False)
```

```python
import functools
import math

import jax
import jax.numpy as jnp
from jax import lax
from jax.experimental import pallas as pl
from jax.experimental.pallas import tpu as pltpu
from jax.sharding import PartitionSpec as P

F32, BF16 = jnp.float32, jnp.bfloat16
OFF = 8
HALO = 4
VMEM_LIMIT = 30 * 1024 * 1024
NT = (((1,), (1,)), ((), ()))
TN = (((0,), (0,)), ((), ()))


def call(kernel, outs, args, scratch=(), smem_args=1, raw_args=(), raw_outs=(), aliases=None):
    def spec(space):
        return pl.BlockSpec(memory_space=space)

    in_specs = [spec(pltpu.SMEM)] * smem_args
    in_specs += [spec(pltpu.HBM if i in raw_args else pltpu.VMEM) for i in range(smem_args, len(args))]
    args = [pltpu.with_memory_space_constraint(a, pltpu.HBM) if i in raw_args else a for i, a in enumerate(args)]
    return pl.pallas_call(
        kernel,
        out_shape=[jax.ShapeDtypeStruct(s, t) for s, t in outs],
        in_specs=in_specs,
        out_specs=[spec(pltpu.HBM if i in raw_outs else pltpu.VMEM) for i in range(len(outs))],
        scratch_shapes=list(scratch),
        input_output_aliases=aliases or {},
        compiler_params=pltpu.CompilerParams(vmem_limit_bytes=VMEM_LIMIT),
    )(*args)


def silu_parts(pre):
    sigma = 1.0 / (1.0 + jnp.exp(-pre))
    return pre * sigma, sigma * (1.0 + pre * (1.0 - sigma))


def after(x, *others):
    return lax.optimization_barrier((x, others))[0]


def row_mask(first, rows, total):
    at = lax.broadcasted_iota(jnp.int32, (rows, 1), 0) + (first - OFF)
    return (at >= 0) & (at < total)


def conv_chunk(x, w, c0, n, backward):
    rows, ch = x.shape[1], x.shape[2]
    sums = []
    for i in range(3):
        total = None
        for j in range(3):
            lhs = x[c0 + j : c0 + j + n].reshape(n * rows, ch)
            if backward:
                term = jnp.dot(lhs, w[(2 - i) * 3 + (2 - j)], preferred_element_type=F32)
            else:
                term = lax.dot_general(lhs, w[i * 3 + j], NT, preferred_element_type=F32)
            total = term if total is None else total + term
        sums.append(total.reshape(n, rows, ch))
    return [pltpu.roll(sums[0][q], 1, 0) + sums[1][q] + pltpu.roll(sums[2][q], rows - 1, 0) for q in range(n)]


def chunks(total, most):
    parts = -(-total // most)
    base, extra = divmod(total, parts)
    out, at = [], 0
    for p in range(parts):
        n = base + (p < extra)
        out.append((at, n))
        at += n
    return out


def assemble_filter(w, own, pieces, iy, ix, ny):
    co = own.shape[1]
    w[:, pl.ds(pl.multiple_of(iy * co, co), co), :] = own[...]
    core, x = lax.rem(ix, 2), lax.rem(lax.div(ix, 2), 2)
    count, size = pieces[0].shape[1], pieces[0].shape[3]
    for d in range(1, ny):
        src = lax.rem(iy - d + ny, ny)
        for p in range(count):
            part = 0 if count == 1 else (x if p == 0 else 1 - x)
            for ref, half in ((pieces[0], core), (pieces[1], 1 - core)):
                at = pl.multiple_of(src * co + half * (co // 2) + part * size, size)
                w[:, pl.ds(at, size), :] = ref[d - 1, p]


def conv1_kernel(dims, where, ft, left, right, up, down, own, mine, other, hidden, slope, fbuf, w):
    ny, hl, wl, height, width = dims
    iy, ix = where[0], where[1]
    rows, ch = fbuf.shape[1], fbuf.shape[2]
    ok = row_mask(iy * hl, rows, height)
    groups, tall = ch // 128, hl + 2 * HALO
    before = jnp.zeros((OFF - HALO, ch), F32)
    after = jnp.zeros((rows - hl - OFF - HALO, ch), F32)
    for c in range(wl + 2 * HALO):
        if HALO <= c < wl + HALO:
            q = c - HALO
            mid = [up[q].astype(F32), ft[q].astype(F32), down[q].astype(F32)]
        else:
            ref, q = (left, c) if c < HALO else (right, c - wl - HALO)
            planes = [ref[(g * HALO + q) * tall : (g * HALO + q + 1) * tall].astype(F32) for g in range(groups)]
            mid = [jnp.concatenate(planes, axis=1)]
        x = jnp.concatenate([before] + mid + [after], axis=0)
        fbuf[c] = jnp.where(ok, x, 0.0).astype(BF16)
    assemble_filter(w, own, (mine, other), iy, ix, ny)
    for c0, n in chunks(wl + 6, 11):
        pre = conv_chunk(fbuf, w, c0, n, False)
        for q in range(n):
            c = c0 + q
            col = ix * wl + c - 3
            act, grad = silu_parts(pre[q])
            inside = ok & (col >= 0) & (col < width)
            hidden[c] = jnp.where(inside, act, 0.0).astype(BF16)
            if 2 <= c < wl + 4:
                slope[c - 2] = jnp.where(inside, grad, 0.0)


def conv2_kernel(dims, where, hidden, own, mine, other, act_out, slope, w):
    ny, hl, wl, height, width = dims
    iy, ix = where[0], where[1]
    rows = hidden.shape[1]
    ok = row_mask(iy * hl, rows, height)
    assemble_filter(w, own, (mine, other), iy, ix, ny)
    for c0, n in chunks(wl + 4, 10):
        pre = conv_chunk(hidden, w, c0, n, False)
        for q in range(n):
            c = c0 + q
            col = ix * wl + c - 2
            act, grad = silu_parts(pre[q])
            inside = ok & (col >= 0) & (col < width)
            slope[c] = jnp.where(inside, grad, 0.0)
            if 2 <= c < wl + 2:
                act_out[c - 2] = act[OFF : OFF + hl].astype(BF16)


def cut_kernel(rows_at, where, features, first, second, cot, edge, send1, send2, low, high, sem):
    iy, ix = where[0], where[1]
    core = lax.rem(ix, 2)
    wl, size = features.shape[1], send1.shape[1]
    at = pl.multiple_of(core * size, size)
    pairs = [(first.at[:, pl.ds(at, size), :], send1), (second.at[:, pl.ds(at, size), :], send2)]
    pairs += [(cot.at[0:2], low), (cot.at[wl - 2 : wl], high)]
    for n, h0 in enumerate(rows_at):
        h0 = jnp.where(iy == 0, h0[0], h0[1])
        pairs.append((features.at[pl.ds(h0, HALO)], edge.at[n]))
    copies = [pltpu.make_async_copy(src, dst, sem.at[n]) for n, (src, dst) in enumerate(pairs)]
    for copy in copies:
        copy.start()
    for copy in copies:
        copy.wait()


def edge_kernel(dims, where, ft, up, down, ct_low, ct_high, low, high):
    ny, hl, wl, height, width = dims
    ch = ft.shape[2]
    groups, tall = ch // 128, hl + 2 * HALO
    for out, first, cot in ((low, 0, ct_low), (high, wl - HALO, ct_high)):
        for q in range(HALO):
            c = first + q
            x = jnp.concatenate([up[c].astype(F32), ft[c].astype(F32), down[c].astype(F32)], axis=0).astype(BF16)
            for g in range(groups):
                at = (g * HALO + q) * tall
                out[at : at + tall] = x[:, g * 128 : (g + 1) * 128]
        out[groups * HALO * tall :] = cot[...].reshape(-1, 128)


def own_rows(rows, hl):
    at = lax.broadcasted_iota(jnp.int32, (rows, 1), 0)
    return (at >= OFF) & (at < OFF + hl)


def put_shifted(shifted, c, grad, own):
    rows, ch = grad.shape
    grad = jnp.where(own, grad, 0.0)
    for i in range(3):
        part = grad if i == 1 else pltpu.roll(grad, (i - 1) % rows, 0)
        shifted[c * rows : (c + 1) * rows, i * ch : (i + 1) * ch] = part.astype(BF16)


def filter_grad(where, x, first, shifted, wl, keep, send):
    low_core = where[1] % 2 == 0
    rows, ch = x.shape[1], x.shape[2]
    half = ch // 2
    for j in range(3):
        rhs = x[first + j : first + j + wl].reshape(wl * rows, ch)
        g = lax.dot_general(shifted[...], rhs, TN, preferred_element_type=F32)
        for i in range(3):
            low, high = g[i * ch : (i + 1) * ch, :half], g[i * ch : (i + 1) * ch, half:]
            keep[i * 3 + j] = jnp.where(low_core, low, high)
            send[i * 3 + j] = jnp.where(low_core, high, low).astype(BF16)


def inner_kernel(dims, count, where, own, mine, other, slope2, slope1, fbuf, *refs):
    cots, (inner, outer, keep, send, w, shifted) = refs[:count], refs[count:]
    ny, hl, wl, height, width = dims
    iy, ix = where[0], where[1]
    rows = fbuf.shape[1]
    mine_rows = own_rows(rows, hl)
    for c in range(wl + 4):
        parts = [ref[c].astype(F32) for ref in cots]
        if len(parts) == 2:
            gap = jnp.zeros((OFF, parts[0].shape[1]), F32)
            a, b = [
                jnp.where(iy == 0, jnp.concatenate([gap, p], axis=0), jnp.concatenate([p, gap], axis=0))
                for p in parts
            ]
            parts = [jnp.where(iy == 0, a, b), jnp.where(iy == 0, b, a)]
        outer[c] = (jnp.concatenate(parts, axis=1) * slope2[c]).astype(BF16)
    assemble_filter(w, own, (mine, other), iy, ix, ny)
    for c0, n in chunks(wl + 2, 9):
        grad = conv_chunk(outer, w, c0, n, True)
        for q in range(n):
            c = c0 + q
            val = (grad[q] * slope1[c]).astype(BF16)
            inner[c] = val
            if 1 <= c < wl + 1:
                put_shifted(shifted, c - 1, val.astype(F32), mine_rows)
    filter_grad(where, fbuf, 3, shifted, wl, keep, send)


def second_grad_kernel(dims, where, hidden, outer, keep, send, shifted):
    ny, hl, wl, height, width = dims
    own = own_rows(hidden.shape[1], hl)
    for c in range(wl):
        put_shifted(shifted, c, outer[c + 2].astype(F32), own)
    filter_grad(where, hidden, 2, shifted, wl, keep, send)


def input_kernel(dims, where, inner, own, mine, other, out, w, flat):
    ny, hl, wl, height, width = dims
    iy, ix = where[0], where[1]
    assemble_filter(w, own, (mine, other), iy, ix, ny)
    for c0, n in chunks(wl, 8):
        grad = conv_chunk(inner, w, c0, n, True)
        for q in range(n):
            for g in range(flat.shape[0]):
                part = grad[q][OFF : OFF + hl, g * 128 : (g + 1) * 128]
                flat[g, pl.ds(c0 + q, hl, stride=wl), :] = part
    for g in range(flat.shape[0]):
        out[:, :, g * 128 : (g + 1) * 128] = flat[g].reshape(hl, wl, 128).astype(BF16)


def split_kernel(blocks, where, keep, came, own, *messages):
    iy, ix = where[0], where[1]
    ny = blocks // 2
    size = keep.shape[1] // blocks
    x = lax.rem(lax.div(ix, 2), 2)

    def block(y, b):
        at = pl.multiple_of((y * 2 + b) * size, size)
        return keep[:, pl.ds(at, size), :] + came[:, pl.ds(at, size), :].astype(F32)

    own[...] = block(iy, x)
    m = 0
    for d in range(ny):
        for b in range(2):
            if d or b:
                y = lax.rem(iy + d, ny)
                messages[m][...] = block(y, x if b == 0 else 1 - x).astype(BF16)
                m += 1


def finish_kernel(scale, where, here, there, out):
    low_core = lax.rem(where[1], 2) == 0
    half = here.shape[2]
    for t in range(here.shape[0]):
        a, b = here[t].astype(F32) * scale, there[t].astype(F32) * scale
        out[t, :, :half] = jnp.where(low_core, a, b)
        out[t, :, half:] = jnp.where(low_core, b, a)


def halving_kernel(where, keep, came, own, other, send):
    iy, ix = where[0], where[1]
    size = own.shape[1]
    x = lax.rem(lax.div(ix, 2), 2)
    by_y = lax.rem(ix, 2) == 0

    def block(y, b):
        at = pl.multiple_of((y * 2 + b) * size, size)
        return keep[:, pl.ds(at, size), :] + came[:, pl.ds(at, size), :].astype(F32)

    own[...] = block(iy, x)
    other[...] = block(jnp.where(by_y, iy, 1 - iy), jnp.where(by_y, 1 - x, x))
    send[:, :size, :] = block(jnp.where(by_y, 1 - iy, iy), jnp.where(by_y, x, 1 - x)).astype(BF16)
    send[:, size:, :] = block(1 - iy, 1 - x).astype(BF16)


def fold_kernel(own, other, came, total, send):
    size = own.shape[1]
    total[...] = own[...] + came[:, :size, :].astype(F32)
    send[...] = (other[...] + came[:, size:, :].astype(F32)).astype(BF16)


def split_filter(where, keep, came, nx, ny):
    blocks = 2 * ny
    taps, ch, half = keep.shape
    shape = (taps, ch // blocks, half)
    if ny == 2:
        outs = [(shape, F32), (shape, F32), ((taps, ch // 2, half), BF16)]
        return call(halving_kernel, outs, (where, keep, came))
    outs = [(shape, F32)] + [(shape, BF16)] * (blocks - 1)
    return call(functools.partial(split_kernel, blocks), outs, (where, keep, came))


def send_planes(parts, nx, ny):
    arrived = []
    for d in range(ny):
        for b in range(2):
            if d or b:
                pairs = [
                    (g * ny + y, (g ^ (2 * b)) * ny + (y + d) % ny) for g in range(nx) for y in range(ny)
                ]
                arrived.append(lax.ppermute(parts[len(arrived) + 1], ("gx", "gy"), pairs))
    return arrived


def halving_pairs(nx, step):
    return [(g * 2 + y, g * 2 + 1 - y if g % 2 == step else (g ^ 2) * 2 + y) for g in range(nx) for y in range(2)]


def add(parts):
    total = parts[0].astype(F32)
    for part in parts[1:]:
        total = total + part.astype(F32)
    return total.astype(BF16)


def far_bits(nx):
    return [1 << b for b in range(2, nx.bit_length() - 1)]


def far_partner(total, step, nx):
    bits = far_bits(nx)
    near, far = bits[step], bits[len(bits) - 1 - step]
    return lax.ppermute(total, "gx", [(g, g ^ (near if g % 2 == 0 else far)) for g in range(nx)])


def finish(where, total, beside, nx, ix, scale):
    first = (ix // 2) % 2 == 0
    here = jnp.concatenate([jnp.where(first, total, beside), jnp.where(first, beside, total)], axis=1)
    there = lax.ppermute(here, "gx", [(g, g ^ 1) for g in range(nx)])
    taps, size, half = here.shape
    (result,) = call(functools.partial(finish_kernel, scale), [((taps, size, 2 * half), F32)], (where, here, there))
    return jnp.transpose(result.reshape(3, 3, size, 2 * half), (2, 0, 1, 3))


def body(features, first_filter, second_filter, cotangent):
    ny, nx = lax.axis_size("gy"), lax.axis_size("gx")
    iy, ix = lax.axis_index("gy"), lax.axis_index("gx")
    hl, wl, ch = features.shape
    co = first_filter.shape[0]
    height, width = hl * ny, wl * nx
    rows = -(-(hl + 2 * OFF) // 16) * 16
    dims = (ny, hl, wl, height, width)
    scale_factor = 1.0 / math.sqrt(height * width)
    where = jnp.stack([iy, ix]).astype(jnp.int32)
    core = ix % 2
    forward = [(i, i + 1) for i in range(nx - 1)]
    backward = [(i + 1, i) for i in range(nx - 1)]

    def round_y(x, d):
        return lax.ppermute(x, "gy", [(i, (i + d) % ny) for i in range(ny)])

    def gathered(taps):
        half = co // 2
        send = lax.dynamic_slice_in_dim(taps, core * half, half, 1)
        mine = jnp.stack([round_y(send, d) for d in range(1, ny)])
        return mine, lax.ppermute(mine, "gx", [(i, i ^ 1) for i in range(nx)])

    def pass_core(mine):
        return lax.ppermute(mine, "gx", [(i, i ^ 1) for i in range(nx)])

    first_own = jnp.transpose(first_filter, (1, 2, 0, 3)).reshape(9, co, ch)
    second_own = jnp.transpose(second_filter, (1, 2, 0, 3)).reshape(9, co, ch)
    ct = jnp.transpose(cotangent, (1, 2, 0))
    groups, tall = ch // 128, hl + 2 * HALO

    half = co // 2
    rows_at = [(hl - HALO, 0)] if ny == 2 else [(hl - HALO, hl - HALO), (0, 0)]
    edge_send, first_send, second_send, ct_low, ct_high = call(
        functools.partial(cut_kernel, rows_at),
        [((len(rows_at), HALO, wl, ch), BF16)] + [((9, half, ch), BF16)] * 2 + [((2, height, co), BF16)] * 2,
        (where, features, first_own, second_own, ct),
        [pltpu.SemaphoreType.DMA((4 + len(rows_at),))],
        raw_args=(1, 2, 3, 4),
    )
    up = jnp.transpose(round_y(edge_send[0], 1), (1, 0, 2))
    down = up if ny == 2 else jnp.transpose(round_y(edge_send[1], ny - 1), (1, 0, 2))

    def spread_y(send):
        return jnp.stack([round_y(send, d) for d in range(1, ny)])[:, None]

    first_mine = spread_y(first_send)

    ft = jnp.transpose(after(features, edge_send), (1, 0, 2))
    at = groups * HALO * tall
    shape = ((at + 2 * height * co // 128, 128), BF16)
    if co % 128:
        ct_low, ct_high = ct_low.reshape(-1, 128), ct_high.reshape(-1, 128)
    low, high = call(functools.partial(edge_kernel, dims), [shape] * 2, (where, ft, up, down, ct_low, ct_high))
    left = lax.ppermute(high, "gx", forward)
    right = lax.ppermute(low, "gx", backward)
    first_mine = after(first_mine, left, right)
    first_in = (first_mine, pass_core(first_mine))
    second_mine = spread_y(after(second_send, low))
    second_in = (second_mine, pass_core(second_mine))

    ct = jnp.concatenate([left[at:].reshape(2, height, co), ct, right[at:].reshape(2, height, co)], axis=0)
    if ny == 2:
        window = hl + OFF
        rows_of = lambda y: lax.dynamic_slice_in_dim(ct, y * (height - window), window, 1)
    else:
        ct = jnp.pad(ct, ((0, 0), (OFF, rows - OFF - hl), (0, 0)))
        rows_of = lambda y: lax.dynamic_slice_in_dim(ct, y * hl, rows, 1)
    cot_send = [rows_of((iy + d) % ny) for d in range(1, ny)]
    ft = after(ft, cot_send, second_mine)
    cots = [rows_of(iy)] + [round_y(cot_send[d - 1], d) for d in range(1, ny)]
    if ny != 2:
        full = jnp.zeros((wl + 4, rows, ch), BF16)
        for d, part in enumerate(cots):
            full = lax.dynamic_update_slice_in_dim(full, part, ((iy - d) % ny) * co, 2)
        cots = [full]

    bf = lambda *s: pltpu.VMEM(s, BF16)
    weights = bf(9, ch, ch)

    fbuf_shape = ((wl + 8, rows, ch), BF16)
    hidden, slope1, fbuf = call(
        functools.partial(conv1_kernel, dims),
        [((wl + 6, rows, ch), BF16), ((wl + 2, rows, ch), F32), fbuf_shape],
        (where, ft, left, right, up, down, first_own, *first_in),
        [weights],
    )
    act, slope2 = call(
        functools.partial(conv2_kernel, dims),
        [((wl, hl, ch), BF16), ((wl + 4, rows, ch), F32)],
        (where, hidden, second_own, *second_in),
        [weights],
    )
    grad_shapes = [((9, ch, ch // 2), F32), ((9, ch, ch // 2), BF16)]
    shifted = bf(wl * rows, 3 * ch)
    inner, outer, keep1, send1 = call(
        functools.partial(inner_kernel, dims, len(cots)),
        [((wl + 2, rows, ch), BF16), ((wl + 4, rows, ch), BF16)] + grad_shapes,
        (where, second_own, *second_in, slope2, slope1, fbuf, *cots),
        [weights, shifted],
    )
    keep2, send2 = call(
        functools.partial(second_grad_kernel, dims),
        grad_shapes,
        (where, hidden, outer),
        [shifted],
    )
    parts1 = split_filter(where, keep1, pass_core(send1), nx, ny)
    parts2 = split_filter(where, after(keep2, parts1), pass_core(send2), nx, ny)
    (input_grad,) = call(
        functools.partial(input_kernel, dims),
        [((hl, wl, ch), BF16)],
        (where, inner, first_own, *first_in),
        [weights, pltpu.VMEM((ch // 128, hl * wl, 128), F32)],
    )
    if ny == 2:
        (own1, other1, send1), (own2, other2, send2) = parts1, parts2
        axes, pairs = ("gx", "gy"), [halving_pairs(nx, step) for step in range(2)]
        came1 = lax.ppermute(send1, axes, pairs[0])
        came2 = lax.ppermute(send2, axes, pairs[0])
        came1 = after(came1, parts2, input_grad)
        shape = own1.shape
        own1, pass1 = call(fold_kernel, [(shape, F32), (shape, BF16)], (own1, other1, came1), smem_args=0)
        own2, pass2 = call(fold_kernel, [(shape, F32), (shape, BF16)], (own2, other2, came2), smem_args=0)
        total1 = add([own1, lax.ppermute(pass1, axes, pairs[1])])
        total2 = add([own2, lax.ppermute(pass2, axes, pairs[1])])
    else:
        total1 = add([after(parts1[0], parts2, input_grad)] + send_planes(parts1, nx, ny))
        total2 = add([parts2[0]] + send_planes(parts2, nx, ny))
    act = after(act, total2)

    def channels_of(y):
        return lax.dynamic_slice_in_dim(act, y * co, co, 2)

    parts = [channels_of(iy)] + [round_y(channels_of((iy + d) % ny), d) for d in range(1, ny)]
    output = jnp.zeros((wl, height, co), BF16)
    for d, part in enumerate(parts):
        output = lax.dynamic_update_slice_in_dim(output, part, ((iy - d) % ny) * hl, 1)
    output = jnp.transpose(output, (2, 0, 1))

    for step in range(len(far_bits(nx))):
        other1 = far_partner(total1, step, nx)
        other2 = far_partner(total2, step, nx)
        total1 = add([total1, other1])
        total2 = add([total2, other2])
    total2 = after(total2, output)
    beside1 = lax.ppermute(total1, "gx", [(g, g ^ 2) for g in range(nx)])
    beside2 = lax.ppermute(total2, "gx", [(g, g ^ 2) for g in range(nx)])
    first_grad = finish(where, total1, beside1, nx, ix, scale_factor)
    second_grad = finish(where, total2, beside2, nx, ix, scale_factor)
    return output, input_grad, first_grad, second_grad


def solution(mesh):
    in_specs = (
        P("gy", "gx", None),
        P("gy", None, None, None),
        P("gy", None, None, None),
        P("gy", "gx", None),
    )
    out_specs = (
        P("gy", "gx", None),
        P("gy", "gx", None),
        P("gy", None, None, None),
        P("gy", None, None, None),
    )
    return jax.shard_map(body, mesh=mesh, in_specs=in_specs, out_specs=out_specs, check_vma=False)
```

```python
import functools
import math

import jax
import jax.numpy as jnp
from jax import lax
from jax.experimental import pallas as pl
from jax.experimental.pallas import tpu as pltpu
from jax.sharding import PartitionSpec as P

F32, BF16 = jnp.float32, jnp.bfloat16
OFF = 8
HALO = 4
VMEM_LIMIT = 30 * 1024 * 1024
NT = (((1,), (1,)), ((), ()))
TN = (((0,), (0,)), ((), ()))


def call(kernel, outs, args, scratch=(), smem_args=1, raw_args=(), raw_outs=(), aliases=None):
    def spec(space):
        return pl.BlockSpec(memory_space=space)

    in_specs = [spec(pltpu.SMEM)] * smem_args
    in_specs += [spec(pltpu.HBM if i in raw_args else pltpu.VMEM) for i in range(smem_args, len(args))]
    args = [pltpu.with_memory_space_constraint(a, pltpu.HBM) if i in raw_args else a for i, a in enumerate(args)]
    return pl.pallas_call(
        kernel,
        out_shape=[jax.ShapeDtypeStruct(s, t) for s, t in outs],
        in_specs=in_specs,
        out_specs=[spec(pltpu.HBM if i in raw_outs else pltpu.VMEM) for i in range(len(outs))],
        scratch_shapes=list(scratch),
        input_output_aliases=aliases or {},
        compiler_params=pltpu.CompilerParams(vmem_limit_bytes=VMEM_LIMIT),
    )(*args)


def silu_parts(pre):
    sigma = 1.0 / (1.0 + jnp.exp(-pre))
    return pre * sigma, sigma * (1.0 + pre * (1.0 - sigma))


def after(x, *others):
    return lax.optimization_barrier((x, others))[0]


def row_mask(first, rows, total):
    at = lax.broadcasted_iota(jnp.int32, (rows, 1), 0) + (first - OFF)
    return (at >= 0) & (at < total)


def conv_chunk(x, w, c0, n, backward):
    rows, ch = x.shape[1], x.shape[2]
    sums = []
    for i in range(3):
        total = None
        for j in range(3):
            lhs = x[c0 + j : c0 + j + n].reshape(n * rows, ch)
            if backward:
                term = jnp.dot(lhs, w[(2 - i) * 3 + (2 - j)], preferred_element_type=F32)
            else:
                term = lax.dot_general(lhs, w[i * 3 + j], NT, preferred_element_type=F32)
            total = term if total is None else total + term
        sums.append(total.reshape(n, rows, ch))
    return [pltpu.roll(sums[0][q], 1, 0) + sums[1][q] + pltpu.roll(sums[2][q], rows - 1, 0) for q in range(n)]


def chunks(total, most):
    parts = -(-total // most)
    base, extra = divmod(total, parts)
    out, at = [], 0
    for p in range(parts):
        n = base + (p < extra)
        out.append((at, n))
        at += n
    return out


def assemble_filter(w, own, pieces, iy, ix, ny):
    co = own.shape[1]
    w[:, pl.ds(pl.multiple_of(iy * co, co), co), :] = own[...]
    core, x = lax.rem(ix, 2), lax.rem(lax.div(ix, 2), 2)
    count, size = pieces[0].shape[1], pieces[0].shape[3]
    for d in range(1, ny):
        src = lax.rem(iy - d + ny, ny)
        for p in range(count):
            part = 0 if count == 1 else (x if p == 0 else 1 - x)
            for ref, half in ((pieces[0], core), (pieces[1], 1 - core)):
                at = pl.multiple_of(src * co + half * (co // 2) + part * size, size)
                w[:, pl.ds(at, size), :] = ref[d - 1, p]


def conv1_kernel(dims, where, ft, left, right, up, down, own, mine, other, hidden, slope, fbuf, w):
    ny, hl, wl, height, width = dims
    iy, ix = where[0], where[1]
    rows, ch = fbuf.shape[1], fbuf.shape[2]
    ok = row_mask(iy * hl, rows, height)
    groups, tall = ch // 128, hl + 2 * HALO
    before = jnp.zeros((OFF - HALO, ch), F32)
    after = jnp.zeros((rows - hl - OFF - HALO, ch), F32)
    for c in range(wl + 2 * HALO):
        if HALO <= c < wl + HALO:
            q = c - HALO
            mid = [up[q].astype(F32), ft[q].astype(F32), down[q].astype(F32)]
        else:
            ref, q = (left, c) if c < HALO else (right, c - wl - HALO)
            planes = [ref[(g * HALO + q) * tall : (g * HALO + q + 1) * tall].astype(F32) for g in range(groups)]
            mid = [jnp.concatenate(planes, axis=1)]
        x = jnp.concatenate([before] + mid + [after], axis=0)
        fbuf[c] = jnp.where(ok, x, 0.0).astype(BF16)
    assemble_filter(w, own, (mine, other), iy, ix, ny)
    for c0, n in chunks(wl + 6, 11):
        pre = conv_chunk(fbuf, w, c0, n, False)
        for q in range(n):
            c = c0 + q
            col = ix * wl + c - 3
            act, grad = silu_parts(pre[q])
            inside = ok & (col >= 0) & (col < width)
            hidden[c] = jnp.where(inside, act, 0.0).astype(BF16)
            if 2 <= c < wl + 4:
                slope[c - 2] = jnp.where(inside, grad, 0.0)


def conv2_kernel(dims, where, hidden, own, mine, other, act_out, slope, w):
    ny, hl, wl, height, width = dims
    iy, ix = where[0], where[1]
    rows = hidden.shape[1]
    ok = row_mask(iy * hl, rows, height)
    assemble_filter(w, own, (mine, other), iy, ix, ny)
    for c0, n in chunks(wl + 4, 10):
        pre = conv_chunk(hidden, w, c0, n, False)
        for q in range(n):
            c = c0 + q
            col = ix * wl + c - 2
            act, grad = silu_parts(pre[q])
            inside = ok & (col >= 0) & (col < width)
            slope[c] = jnp.where(inside, grad, 0.0)
            if 2 <= c < wl + 2:
                act_out[c - 2] = act[OFF : OFF + hl].astype(BF16)


def cut_kernel(rows_at, where, features, first, second, cot, edge, send1, send2, low, high, sem):
    iy, ix = where[0], where[1]
    core = lax.rem(ix, 2)
    wl, size = features.shape[1], send1.shape[1]
    at = pl.multiple_of(core * size, size)
    pairs = [(first.at[:, pl.ds(at, size), :], send1), (second.at[:, pl.ds(at, size), :], send2)]
    pairs += [(cot.at[0:2], low), (cot.at[wl - 2 : wl], high)]
    for n, h0 in enumerate(rows_at):
        h0 = jnp.where(iy == 0, h0[0], h0[1])
        pairs.append((features.at[pl.ds(h0, HALO)], edge.at[n]))
    copies = [pltpu.make_async_copy(src, dst, sem.at[n]) for n, (src, dst) in enumerate(pairs)]
    for copy in copies:
        copy.start()
    for copy in copies:
        copy.wait()


def edge_kernel(dims, where, ft, up, down, ct_low, ct_high, low, high):
    ny, hl, wl, height, width = dims
    ch = ft.shape[2]
    groups, tall = ch // 128, hl + 2 * HALO
    for out, first, cot in ((low, 0, ct_low), (high, wl - HALO, ct_high)):
        for q in range(HALO):
            c = first + q
            x = jnp.concatenate([up[c].astype(F32), ft[c].astype(F32), down[c].astype(F32)], axis=0).astype(BF16)
            for g in range(groups):
                at = (g * HALO + q) * tall
                out[at : at + tall] = x[:, g * 128 : (g + 1) * 128]
        out[groups * HALO * tall :] = cot[...].reshape(-1, 128)


def own_rows(rows, hl):
    at = lax.broadcasted_iota(jnp.int32, (rows, 1), 0)
    return (at >= OFF) & (at < OFF + hl)


def put_shifted(shifted, c, grad, own):
    rows, ch = grad.shape
    grad = jnp.where(own, grad, 0.0)
    for i in range(3):
        part = grad if i == 1 else pltpu.roll(grad, (i - 1) % rows, 0)
        shifted[c * rows : (c + 1) * rows, i * ch : (i + 1) * ch] = part.astype(BF16)


def filter_grad(where, x, first, shifted, wl, keep, send):
    low_core = where[1] % 2 == 0
    rows, ch = x.shape[1], x.shape[2]
    half = ch // 2
    for j in range(3):
        rhs = x[first + j : first + j + wl].reshape(wl * rows, ch)
        g = lax.dot_general(shifted[...], rhs, TN, preferred_element_type=F32)
        for i in range(3):
            low, high = g[i * ch : (i + 1) * ch, :half], g[i * ch : (i + 1) * ch, half:]
            keep[i * 3 + j] = jnp.where(low_core, low, high)
            send[i * 3 + j] = jnp.where(low_core, high, low).astype(BF16)


def inner_kernel(dims, count, where, w, slope2, slope1, fbuf, *refs):
    cots, (inner, outer, keep, send, shifted) = refs[:count], refs[count:]
    ny, hl, wl, height, width = dims
    iy, ix = where[0], where[1]
    rows = fbuf.shape[1]
    mine_rows = own_rows(rows, hl)
    for c in range(wl + 4):
        parts = [ref[c].astype(F32) for ref in cots]
        if len(parts) == 2:
            gap = jnp.zeros((OFF, parts[0].shape[1]), F32)
            a, b = [
                jnp.where(iy == 0, jnp.concatenate([gap, p], axis=0), jnp.concatenate([p, gap], axis=0))
                for p in parts
            ]
            parts = [jnp.where(iy == 0, a, b), jnp.where(iy == 0, b, a)]
        outer[c] = (jnp.concatenate(parts, axis=1) * slope2[c]).astype(BF16)
    for c0, n in chunks(wl + 2, 9):
        grad = conv_chunk(outer, w, c0, n, True)
        for q in range(n):
            c = c0 + q
            val = (grad[q] * slope1[c]).astype(BF16)
            inner[c] = val
            if 1 <= c < wl + 1:
                put_shifted(shifted, c - 1, val.astype(F32), mine_rows)
    filter_grad(where, fbuf, 3, shifted, wl, keep, send)


def second_grad_kernel(dims, where, hidden, outer, keep, send, shifted):
    ny, hl, wl, height, width = dims
    own = own_rows(hidden.shape[1], hl)
    for c in range(wl):
        put_shifted(shifted, c, outer[c + 2].astype(F32), own)
    filter_grad(where, hidden, 2, shifted, wl, keep, send)


def input_kernel(dims, where, inner, own, mine, other, out, w, flat):
    ny, hl, wl, height, width = dims
    iy, ix = where[0], where[1]
    assemble_filter(w, own, (mine, other), iy, ix, ny)
    for c0, n in chunks(wl, 8):
        grad = conv_chunk(inner, w, c0, n, True)
        for q in range(n):
            for g in range(flat.shape[0]):
                part = grad[q][OFF : OFF + hl, g * 128 : (g + 1) * 128]
                flat[g, pl.ds(c0 + q, hl, stride=wl), :] = part
    for g in range(flat.shape[0]):
        out[:, :, g * 128 : (g + 1) * 128] = flat[g].reshape(hl, wl, 128).astype(BF16)


def split_kernel(blocks, where, keep, came, own, *messages):
    iy, ix = where[0], where[1]
    ny = blocks // 2
    size = keep.shape[1] // blocks
    x = lax.rem(lax.div(ix, 2), 2)

    def block(y, b):
        at = pl.multiple_of((y * 2 + b) * size, size)
        return keep[:, pl.ds(at, size), :] + came[:, pl.ds(at, size), :].astype(F32)

    own[...] = block(iy, x)
    m = 0
    for d in range(ny):
        for b in range(2):
            if d or b:
                y = lax.rem(iy + d, ny)
                messages[m][...] = block(y, x if b == 0 else 1 - x).astype(BF16)
                m += 1


def finish_kernel(scale, where, here, there, out):
    low_core = lax.rem(where[1], 2) == 0
    half = here.shape[2]
    for t in range(here.shape[0]):
        a, b = here[t].astype(F32) * scale, there[t].astype(F32) * scale
        out[t, :, :half] = jnp.where(low_core, a, b)
        out[t, :, half:] = jnp.where(low_core, b, a)


def halving_kernel(where, keep, came, own, other, send):
    iy, ix = where[0], where[1]
    size = own.shape[1]
    x = lax.rem(lax.div(ix, 2), 2)
    by_y = lax.rem(ix, 2) == 0

    def block(y, b):
        at = pl.multiple_of((y * 2 + b) * size, size)
        return keep[:, pl.ds(at, size), :] + came[:, pl.ds(at, size), :].astype(F32)

    own[...] = block(iy, x)
    other[...] = block(jnp.where(by_y, iy, 1 - iy), jnp.where(by_y, 1 - x, x))
    send[:, :size, :] = block(jnp.where(by_y, 1 - iy, iy), jnp.where(by_y, x, 1 - x)).astype(BF16)
    send[:, size:, :] = block(1 - iy, 1 - x).astype(BF16)


def fold_kernel(own, other, came, total, send):
    size = own.shape[1]
    total[...] = own[...] + came[:, :size, :].astype(F32)
    send[...] = (other[...] + came[:, size:, :].astype(F32)).astype(BF16)


def split_filter(where, keep, came, nx, ny):
    blocks = 2 * ny
    taps, ch, half = keep.shape
    shape = (taps, ch // blocks, half)
    if ny == 2:
        outs = [(shape, F32), (shape, F32), ((taps, ch // 2, half), BF16)]
        return call(halving_kernel, outs, (where, keep, came))
    outs = [(shape, F32)] + [(shape, BF16)] * (blocks - 1)
    return call(functools.partial(split_kernel, blocks), outs, (where, keep, came))


def send_planes(parts, nx, ny):
    arrived = []
    for d in range(ny):
        for b in range(2):
            if d or b:
                pairs = [
                    (g * ny + y, (g ^ (2 * b)) * ny + (y + d) % ny) for g in range(nx) for y in range(ny)
                ]
                arrived.append(lax.ppermute(parts[len(arrived) + 1], ("gx", "gy"), pairs))
    return arrived


def halving_pairs(nx, step):
    return [(g * 2 + y, g * 2 + 1 - y if g % 2 == step else (g ^ 2) * 2 + y) for g in range(nx) for y in range(2)]


def add(parts):
    total = parts[0].astype(F32)
    for part in parts[1:]:
        total = total + part.astype(F32)
    return total.astype(BF16)


def far_bits(nx):
    return [1 << b for b in range(2, nx.bit_length() - 1)]


def far_partner(total, step, nx):
    bits = far_bits(nx)
    near, far = bits[step], bits[len(bits) - 1 - step]
    return lax.ppermute(total, "gx", [(g, g ^ (near if g % 2 == 0 else far)) for g in range(nx)])


def finish(where, total, beside, nx, ix, scale):
    first = (ix // 2) % 2 == 0
    here = jnp.concatenate([jnp.where(first, total, beside), jnp.where(first, beside, total)], axis=1)
    there = lax.ppermute(here, "gx", [(g, g ^ 1) for g in range(nx)])
    taps, size, half = here.shape
    (result,) = call(functools.partial(finish_kernel, scale), [((taps, size, 2 * half), F32)], (where, here, there))
    return jnp.transpose(result.reshape(3, 3, size, 2 * half), (2, 0, 1, 3))


def body(features, first_filter, second_filter, cotangent):
    ny, nx = lax.axis_size("gy"), lax.axis_size("gx")
    iy, ix = lax.axis_index("gy"), lax.axis_index("gx")
    hl, wl, ch = features.shape
    co = first_filter.shape[0]
    height, width = hl * ny, wl * nx
    rows = -(-(hl + 2 * OFF) // 16) * 16
    dims = (ny, hl, wl, height, width)
    scale_factor = 1.0 / math.sqrt(height * width)
    where = jnp.stack([iy, ix]).astype(jnp.int32)
    core = ix % 2
    forward = [(i, i + 1) for i in range(nx - 1)]
    backward = [(i + 1, i) for i in range(nx - 1)]

    def round_y(x, d):
        return lax.ppermute(x, "gy", [(i, (i + d) % ny) for i in range(ny)])

    def gathered(taps):
        half = co // 2
        send = lax.dynamic_slice_in_dim(taps, core * half, half, 1)
        mine = jnp.stack([round_y(send, d) for d in range(1, ny)])
        return mine, lax.ppermute(mine, "gx", [(i, i ^ 1) for i in range(nx)])

    def pass_core(mine):
        return lax.ppermute(mine, "gx", [(i, i ^ 1) for i in range(nx)])

    first_own = jnp.transpose(first_filter, (1, 2, 0, 3)).reshape(9, co, ch)
    second_own = jnp.transpose(second_filter, (1, 2, 0, 3)).reshape(9, co, ch)
    ct = jnp.transpose(cotangent, (1, 2, 0))
    groups, tall = ch // 128, hl + 2 * HALO

    half = co // 2
    rows_at = [(hl - HALO, 0)] if ny == 2 else [(hl - HALO, hl - HALO), (0, 0)]
    edge_send, first_send, second_send, ct_low, ct_high = call(
        functools.partial(cut_kernel, rows_at),
        [((len(rows_at), HALO, wl, ch), BF16)] + [((9, half, ch), BF16)] * 2 + [((2, height, co), BF16)] * 2,
        (where, features, first_own, second_own, ct),
        [pltpu.SemaphoreType.DMA((4 + len(rows_at),))],
        raw_args=(1, 2, 3, 4),
    )
    up = jnp.transpose(round_y(edge_send[0], 1), (1, 0, 2))
    down = up if ny == 2 else jnp.transpose(round_y(edge_send[1], ny - 1), (1, 0, 2))

    def spread_y(send):
        return jnp.stack([round_y(send, d) for d in range(1, ny)])[:, None]

    first_mine = spread_y(first_send)

    ft = jnp.transpose(after(features, edge_send), (1, 0, 2))
    at = groups * HALO * tall
    shape = ((at + 2 * height * co // 128, 128), BF16)
    if co % 128:
        ct_low, ct_high = ct_low.reshape(-1, 128), ct_high.reshape(-1, 128)
    low, high = call(functools.partial(edge_kernel, dims), [shape] * 2, (where, ft, up, down, ct_low, ct_high))
    left = lax.ppermute(high, "gx", forward)
    right = lax.ppermute(low, "gx", backward)
    first_mine = after(first_mine, left, right)
    first_in = (first_mine, pass_core(first_mine))
    second_mine = spread_y(after(second_send, up))
    second_in = (second_mine, pass_core(second_mine))

    ct = jnp.concatenate([left[at:].reshape(2, height, co), ct, right[at:].reshape(2, height, co)], axis=0)
    if ny == 2:
        window = hl + OFF
        rows_of = lambda y: lax.dynamic_slice_in_dim(ct, y * (height - window), window, 1)
    else:
        ct = jnp.pad(ct, ((0, 0), (OFF, rows - OFF - hl), (0, 0)))
        rows_of = lambda y: lax.dynamic_slice_in_dim(ct, y * hl, rows, 1)
    cot_send = [rows_of((iy + d) % ny) for d in range(1, ny)]
    ft = after(ft, cot_send, second_mine)
    cots = [rows_of(iy)] + [round_y(cot_send[d - 1], d) for d in range(1, ny)]
    if ny != 2:
        full = jnp.zeros((wl + 4, rows, ch), BF16)
        for d, part in enumerate(cots):
            full = lax.dynamic_update_slice_in_dim(full, part, ((iy - d) % ny) * co, 2)
        cots = [full]

    bf = lambda *s: pltpu.VMEM(s, BF16)
    weights = bf(9, ch, ch)

    fbuf_shape = ((wl + 8, rows, ch), BF16)
    hidden, slope1, fbuf = call(
        functools.partial(conv1_kernel, dims),
        [((wl + 6, rows, ch), BF16), ((wl + 2, rows, ch), F32), fbuf_shape],
        (where, ft, left, right, up, down, first_own, *first_in),
        [weights],
    )
    act, slope2, second_all = call(
        functools.partial(conv2_kernel, dims),
        [((wl, hl, ch), BF16), ((wl + 4, rows, ch), F32), ((9, ch, ch), BF16)],
        (where, hidden, second_own, *second_in),
    )
    grad_shapes = [((9, ch, ch // 2), F32), ((9, ch, ch // 2), BF16)]
    shifted = bf(wl * rows, 3 * ch)
    inner, outer, keep1, send1 = call(
        functools.partial(inner_kernel, dims, len(cots)),
        [((wl + 2, rows, ch), BF16), ((wl + 4, rows, ch), BF16)] + grad_shapes,
        (where, second_all, slope2, slope1, fbuf, *cots),
        [shifted],
    )
    keep2, send2 = call(
        functools.partial(second_grad_kernel, dims),
        grad_shapes,
        (where, hidden, outer),
        [shifted],
    )
    parts1 = split_filter(where, keep1, pass_core(send1), nx, ny)
    parts2 = split_filter(where, after(keep2, parts1), pass_core(send2), nx, ny)
    (input_grad,) = call(
        functools.partial(input_kernel, dims),
        [((hl, wl, ch), BF16)],
        (where, inner, first_own, *first_in),
        [weights, pltpu.VMEM((ch // 128, hl * wl, 128), F32)],
    )
    if ny == 2:
        (own1, other1, send1), (own2, other2, send2) = parts1, parts2
        axes, pairs = ("gx", "gy"), [halving_pairs(nx, step) for step in range(2)]
        came1 = lax.ppermute(send1, axes, pairs[0])
        came2 = lax.ppermute(send2, axes, pairs[0])
        came1 = after(came1, parts2, input_grad)
        shape = own1.shape
        own1, pass1 = call(fold_kernel, [(shape, F32), (shape, BF16)], (own1, other1, came1), smem_args=0)
        own2, pass2 = call(fold_kernel, [(shape, F32), (shape, BF16)], (own2, other2, came2), smem_args=0)
        total1 = add([own1, lax.ppermute(pass1, axes, pairs[1])])
        total2 = add([own2, lax.ppermute(pass2, axes, pairs[1])])
    else:
        total1 = add([after(parts1[0], parts2, input_grad)] + send_planes(parts1, nx, ny))
        total2 = add([parts2[0]] + send_planes(parts2, nx, ny))
    act = after(act, total1)

    def channels_of(y):
        return lax.dynamic_slice_in_dim(act, y * co, co, 2)

    parts = [channels_of(iy)] + [round_y(channels_of((iy + d) % ny), d) for d in range(1, ny)]
    output = jnp.zeros((wl, height, co), BF16)
    for d, part in enumerate(parts):
        output = lax.dynamic_update_slice_in_dim(output, part, ((iy - d) % ny) * hl, 1)
    output = jnp.transpose(output, (2, 0, 1))

    for step in range(len(far_bits(nx))):
        other1 = far_partner(total1, step, nx)
        other2 = far_partner(total2, step, nx)
        total1 = add([total1, other1])
        total2 = add([total2, other2])
    total2 = after(total2, output)
    beside1 = lax.ppermute(total1, "gx", [(g, g ^ 2) for g in range(nx)])
    beside2 = lax.ppermute(total2, "gx", [(g, g ^ 2) for g in range(nx)])
    first_grad = finish(where, total1, beside1, nx, ix, scale_factor)
    second_grad = finish(where, total2, beside2, nx, ix, scale_factor)
    return output, input_grad, first_grad, second_grad


def solution(mesh):
    in_specs = (
        P("gy", "gx", None),
        P("gy", None, None, None),
        P("gy", None, None, None),
        P("gy", "gx", None),
    )
    out_specs = (
        P("gy", "gx", None),
        P("gy", "gx", None),
        P("gy", None, None, None),
        P("gy", None, None, None),
    )
    return jax.shard_map(body, mesh=mesh, in_specs=in_specs, out_specs=out_specs, check_vma=False)
```

```python
import functools
import math

import jax
import jax.numpy as jnp
from jax import lax
from jax.experimental import pallas as pl
from jax.experimental.pallas import tpu as pltpu
from jax.sharding import PartitionSpec as P

F32, BF16 = jnp.float32, jnp.bfloat16
OFF = 8
HALO = 4
VMEM_LIMIT = 30 * 1024 * 1024
NT = (((1,), (1,)), ((), ()))
TN = (((0,), (0,)), ((), ()))


def call(kernel, outs, args, scratch=(), smem_args=1, raw_args=(), raw_outs=(), aliases=None):
    def spec(space):
        return pl.BlockSpec(memory_space=space)

    in_specs = [spec(pltpu.SMEM)] * smem_args
    in_specs += [spec(pltpu.HBM if i in raw_args else pltpu.VMEM) for i in range(smem_args, len(args))]
    args = [pltpu.with_memory_space_constraint(a, pltpu.HBM) if i in raw_args else a for i, a in enumerate(args)]
    return pl.pallas_call(
        kernel,
        out_shape=[jax.ShapeDtypeStruct(s, t) for s, t in outs],
        in_specs=in_specs,
        out_specs=[spec(pltpu.HBM if i in raw_outs else pltpu.VMEM) for i in range(len(outs))],
        scratch_shapes=list(scratch),
        input_output_aliases=aliases or {},
        compiler_params=pltpu.CompilerParams(vmem_limit_bytes=VMEM_LIMIT),
    )(*args)


def silu_parts(pre):
    sigma = 1.0 / (1.0 + jnp.exp(-pre))
    return pre * sigma, sigma * (1.0 + pre * (1.0 - sigma))


def after(x, *others):
    return lax.optimization_barrier((x, others))[0]


def row_mask(first, rows, total):
    at = lax.broadcasted_iota(jnp.int32, (rows, 1), 0) + (first - OFF)
    return (at >= 0) & (at < total)


def conv_chunk(x, w, c0, n, backward):
    rows, ch = x.shape[1], x.shape[2]
    sums = []
    for i in range(3):
        total = None
        for j in range(3):
            lhs = x[c0 + j : c0 + j + n].reshape(n * rows, ch)
            if backward:
                term = jnp.dot(lhs, w[(2 - i) * 3 + (2 - j)], preferred_element_type=F32)
            else:
                term = lax.dot_general(lhs, w[i * 3 + j], NT, preferred_element_type=F32)
            total = term if total is None else total + term
        sums.append(total.reshape(n, rows, ch))
    return [pltpu.roll(sums[0][q], 1, 0) + sums[1][q] + pltpu.roll(sums[2][q], rows - 1, 0) for q in range(n)]


def chunks(total, most):
    parts = -(-total // most)
    base, extra = divmod(total, parts)
    out, at = [], 0
    for p in range(parts):
        n = base + (p < extra)
        out.append((at, n))
        at += n
    return out


def assemble_filter(w, own, pieces, iy, ix, ny):
    co = own.shape[1]
    w[:, pl.ds(pl.multiple_of(iy * co, co), co), :] = own[...]
    core, x = lax.rem(ix, 2), lax.rem(lax.div(ix, 2), 2)
    count, size = pieces[0].shape[1], pieces[0].shape[3]
    for d in range(1, ny):
        src = lax.rem(iy - d + ny, ny)
        for p in range(count):
            part = 0 if count == 1 else (x if p == 0 else 1 - x)
            for ref, half in ((pieces[0], core), (pieces[1], 1 - core)):
                at = pl.multiple_of(src * co + half * (co // 2) + part * size, size)
                w[:, pl.ds(at, size), :] = ref[d - 1, p]


def conv1_kernel(dims, where, ft, left, right, up, down, own, mine, other, hidden, slope, fbuf, w):
    ny, hl, wl, height, width = dims
    iy, ix = where[0], where[1]
    rows, ch = fbuf.shape[1], fbuf.shape[2]
    ok = row_mask(iy * hl, rows, height)
    groups, tall = ch // 128, hl + 2 * HALO
    before = jnp.zeros((OFF - HALO, ch), F32)
    after = jnp.zeros((rows - hl - OFF - HALO, ch), F32)
    for c in range(wl + 2 * HALO):
        if HALO <= c < wl + HALO:
            q = c - HALO
            mid = [up[q].astype(F32), ft[q].astype(F32), down[q].astype(F32)]
        else:
            ref, q = (left, c) if c < HALO else (right, c - wl - HALO)
            planes = [ref[(g * HALO + q) * tall : (g * HALO + q + 1) * tall].astype(F32) for g in range(groups)]
            mid = [jnp.concatenate(planes, axis=1)]
        x = jnp.concatenate([before] + mid + [after], axis=0)
        fbuf[c] = jnp.where(ok, x, 0.0).astype(BF16)
    assemble_filter(w, own, (mine, other), iy, ix, ny)
    for c0, n in chunks(wl + 6, 11):
        pre = conv_chunk(fbuf, w, c0, n, False)
        for q in range(n):
            c = c0 + q
            col = ix * wl + c - 3
            act, grad = silu_parts(pre[q])
            inside = ok & (col >= 0) & (col < width)
            hidden[c] = jnp.where(inside, act, 0.0).astype(BF16)
            if 2 <= c < wl + 4:
                slope[c - 2] = jnp.where(inside, grad, 0.0)


def conv2_kernel(dims, where, hidden, own, mine, other, act_out, slope, w):
    ny, hl, wl, height, width = dims
    iy, ix = where[0], where[1]
    rows = hidden.shape[1]
    ok = row_mask(iy * hl, rows, height)
    assemble_filter(w, own, (mine, other), iy, ix, ny)
    for c0, n in chunks(wl + 4, 10):
        pre = conv_chunk(hidden, w, c0, n, False)
        for q in range(n):
            c = c0 + q
            col = ix * wl + c - 2
            act, grad = silu_parts(pre[q])
            inside = ok & (col >= 0) & (col < width)
            slope[c] = jnp.where(inside, grad, 0.0)
            if 2 <= c < wl + 2:
                act_out[c - 2] = act[OFF : OFF + hl].astype(BF16)


def run_copies(pairs, sem):
    copies = [pltpu.make_async_copy(src, dst, sem.at[n]) for n, (src, dst) in enumerate(pairs)]
    for copy in copies:
        copy.start()
    for copy in copies:
        copy.wait()


def cut_kernel(rows_at, where, features, first, edge, send, sem):
    iy, ix = where[0], where[1]
    size = send.shape[1]
    at = pl.multiple_of(lax.rem(ix, 2) * size, size)
    pairs = [(first.at[:, pl.ds(at, size), :], send)]
    for n, h0 in enumerate(rows_at):
        h0 = jnp.where(iy == 0, h0[0], h0[1])
        pairs.append((features.at[pl.ds(h0, HALO)], edge.at[n]))
    run_copies(pairs, sem)


def cut_later_kernel(where, second, cot, send, low, high, sem):
    size, wl = send.shape[1], cot.shape[0]
    at = pl.multiple_of(lax.rem(where[1], 2) * size, size)
    run_copies([(second.at[:, pl.ds(at, size), :], send), (cot.at[0:2], low), (cot.at[wl - 2 : wl], high)], sem)


def edge_kernel(dims, where, ft, up, down, ct_low, ct_high, low, high):
    ny, hl, wl, height, width = dims
    ch = ft.shape[2]
    groups, tall = ch // 128, hl + 2 * HALO
    for out, first, cot in ((low, 0, ct_low), (high, wl - HALO, ct_high)):
        for q in range(HALO):
            c = first + q
            x = jnp.concatenate([up[c].astype(F32), ft[c].astype(F32), down[c].astype(F32)], axis=0).astype(BF16)
            for g in range(groups):
                at = (g * HALO + q) * tall
                out[at : at + tall] = x[:, g * 128 : (g + 1) * 128]
        out[groups * HALO * tall :] = cot[...].reshape(-1, 128)


def own_rows(rows, hl):
    at = lax.broadcasted_iota(jnp.int32, (rows, 1), 0)
    return (at >= OFF) & (at < OFF + hl)


def put_shifted(shifted, c, grad, own):
    rows, ch = grad.shape
    grad = jnp.where(own, grad, 0.0)
    for i in range(3):
        part = grad if i == 1 else pltpu.roll(grad, (i - 1) % rows, 0)
        shifted[c * rows : (c + 1) * rows, i * ch : (i + 1) * ch] = part.astype(BF16)


def filter_grad(where, x, first, shifted, wl, keep, send):
    low_core = where[1] % 2 == 0
    rows, ch = x.shape[1], x.shape[2]
    half = ch // 2
    for j in range(3):
        rhs = x[first + j : first + j + wl].reshape(wl * rows, ch)
        g = lax.dot_general(shifted[...], rhs, TN, preferred_element_type=F32)
        for i in range(3):
            low, high = g[i * ch : (i + 1) * ch, :half], g[i * ch : (i + 1) * ch, half:]
            keep[i * 3 + j] = jnp.where(low_core, low, high)
            send[i * 3 + j] = jnp.where(low_core, high, low).astype(BF16)


def inner_kernel(dims, count, where, w, slope2, slope1, fbuf, *refs):
    cots, (inner, outer, keep, send, shifted) = refs[:count], refs[count:]
    ny, hl, wl, height, width = dims
    iy, ix = where[0], where[1]
    rows = fbuf.shape[1]
    mine_rows = own_rows(rows, hl)
    for c in range(wl + 4):
        parts = [ref[c].astype(F32) for ref in cots]
        if len(parts) == 2:
            gap = jnp.zeros((OFF, parts[0].shape[1]), F32)
            a, b = [
                jnp.where(iy == 0, jnp.concatenate([gap, p], axis=0), jnp.concatenate([p, gap], axis=0))
                for p in parts
            ]
            parts = [jnp.where(iy == 0, a, b), jnp.where(iy == 0, b, a)]
        outer[c] = (jnp.concatenate(parts, axis=1) * slope2[c]).astype(BF16)
    for c0, n in chunks(wl + 2, 9):
        grad = conv_chunk(outer, w, c0, n, True)
        for q in range(n):
            c = c0 + q
            val = (grad[q] * slope1[c]).astype(BF16)
            inner[c] = val
            if 1 <= c < wl + 1:
                put_shifted(shifted, c - 1, val.astype(F32), mine_rows)
    filter_grad(where, fbuf, 3, shifted, wl, keep, send)


def second_grad_kernel(dims, where, hidden, outer, keep, send, shifted):
    ny, hl, wl, height, width = dims
    own = own_rows(hidden.shape[1], hl)
    for c in range(wl):
        put_shifted(shifted, c, outer[c + 2].astype(F32), own)
    filter_grad(where, hidden, 2, shifted, wl, keep, send)


def input_kernel(dims, where, inner, own, mine, other, out, w, flat):
    ny, hl, wl, height, width = dims
    iy, ix = where[0], where[1]
    assemble_filter(w, own, (mine, other), iy, ix, ny)
    for c0, n in chunks(wl, 8):
        grad = conv_chunk(inner, w, c0, n, True)
        for q in range(n):
            for g in range(flat.shape[0]):
                part = grad[q][OFF : OFF + hl, g * 128 : (g + 1) * 128]
                flat[g, pl.ds(c0 + q, hl, stride=wl), :] = part
    for g in range(flat.shape[0]):
        out[:, :, g * 128 : (g + 1) * 128] = flat[g].reshape(hl, wl, 128).astype(BF16)


def split_kernel(blocks, where, keep, came, own, *messages):
    iy, ix = where[0], where[1]
    ny = blocks // 2
    size = keep.shape[1] // blocks
    x = lax.rem(lax.div(ix, 2), 2)

    def block(y, b):
        at = pl.multiple_of((y * 2 + b) * size, size)
        return keep[:, pl.ds(at, size), :] + came[:, pl.ds(at, size), :].astype(F32)

    own[...] = block(iy, x)
    m = 0
    for d in range(ny):
        for b in range(2):
            if d or b:
                y = lax.rem(iy + d, ny)
                messages[m][...] = block(y, x if b == 0 else 1 - x).astype(BF16)
                m += 1


def finish_kernel(scale, where, here, there, out):
    low_core = lax.rem(where[1], 2) == 0
    half = here.shape[2]
    for t in range(here.shape[0]):
        a, b = here[t].astype(F32) * scale, there[t].astype(F32) * scale
        out[t, :, :half] = jnp.where(low_core, a, b)
        out[t, :, half:] = jnp.where(low_core, b, a)


def halving_kernel(where, keep, came, own, other, send):
    iy, ix = where[0], where[1]
    size = own.shape[1]
    x = lax.rem(lax.div(ix, 2), 2)
    by_y = lax.rem(ix, 2) == 0

    def block(y, b):
        at = pl.multiple_of((y * 2 + b) * size, size)
        return keep[:, pl.ds(at, size), :] + came[:, pl.ds(at, size), :].astype(F32)

    own[...] = block(iy, x)
    other[...] = block(jnp.where(by_y, iy, 1 - iy), jnp.where(by_y, 1 - x, x))
    send[:, :size, :] = block(jnp.where(by_y, 1 - iy, iy), jnp.where(by_y, x, 1 - x)).astype(BF16)
    send[:, size:, :] = block(1 - iy, 1 - x).astype(BF16)


def fold_kernel(own, other, came, total, send):
    size = own.shape[1]
    total[...] = own[...] + came[:, :size, :].astype(F32)
    send[...] = (other[...] + came[:, size:, :].astype(F32)).astype(BF16)


def split_filter(where, keep, came, nx, ny):
    blocks = 2 * ny
    taps, ch, half = keep.shape
    shape = (taps, ch // blocks, half)
    if ny == 2:
        outs = [(shape, F32), (shape, F32), ((taps, ch // 2, half), BF16)]
        return call(halving_kernel, outs, (where, keep, came))
    outs = [(shape, F32)] + [(shape, BF16)] * (blocks - 1)
    return call(functools.partial(split_kernel, blocks), outs, (where, keep, came))


def send_planes(parts, nx, ny):
    arrived = []
    for d in range(ny):
        for b in range(2):
            if d or b:
                pairs = [
                    (g * ny + y, (g ^ (2 * b)) * ny + (y + d) % ny) for g in range(nx) for y in range(ny)
                ]
                arrived.append(lax.ppermute(parts[len(arrived) + 1], ("gx", "gy"), pairs))
    return arrived


def halving_pairs(nx, step):
    return [(g * 2 + y, g * 2 + 1 - y if g % 2 == step else (g ^ 2) * 2 + y) for g in range(nx) for y in range(2)]


def add(parts):
    total = parts[0].astype(F32)
    for part in parts[1:]:
        total = total + part.astype(F32)
    return total.astype(BF16)


def far_bits(nx):
    return [1 << b for b in range(2, nx.bit_length() - 1)]


def far_partner(total, step, nx):
    bits = far_bits(nx)
    near, far = bits[step], bits[len(bits) - 1 - step]
    return lax.ppermute(total, "gx", [(g, g ^ (near if g % 2 == 0 else far)) for g in range(nx)])


def finish(where, total, beside, nx, ix, scale):
    first = (ix // 2) % 2 == 0
    here = jnp.concatenate([jnp.where(first, total, beside), jnp.where(first, beside, total)], axis=1)
    there = lax.ppermute(here, "gx", [(g, g ^ 1) for g in range(nx)])
    taps, size, half = here.shape
    (result,) = call(functools.partial(finish_kernel, scale), [((taps, size, 2 * half), F32)], (where, here, there))
    return jnp.transpose(result.reshape(3, 3, size, 2 * half), (2, 0, 1, 3))


def body(features, first_filter, second_filter, cotangent):
    ny, nx = lax.axis_size("gy"), lax.axis_size("gx")
    iy, ix = lax.axis_index("gy"), lax.axis_index("gx")
    hl, wl, ch = features.shape
    co = first_filter.shape[0]
    height, width = hl * ny, wl * nx
    rows = -(-(hl + 2 * OFF) // 16) * 16
    dims = (ny, hl, wl, height, width)
    scale_factor = 1.0 / math.sqrt(height * width)
    where = jnp.stack([iy, ix]).astype(jnp.int32)
    core = ix % 2
    forward = [(i, i + 1) for i in range(nx - 1)]
    backward = [(i + 1, i) for i in range(nx - 1)]

    def round_y(x, d):
        return lax.ppermute(x, "gy", [(i, (i + d) % ny) for i in range(ny)])

    def gathered(taps):
        half = co // 2
        send = lax.dynamic_slice_in_dim(taps, core * half, half, 1)
        mine = jnp.stack([round_y(send, d) for d in range(1, ny)])
        return mine, lax.ppermute(mine, "gx", [(i, i ^ 1) for i in range(nx)])

    def pass_core(mine):
        return lax.ppermute(mine, "gx", [(i, i ^ 1) for i in range(nx)])

    first_own = jnp.transpose(first_filter, (1, 2, 0, 3)).reshape(9, co, ch)
    second_own = jnp.transpose(second_filter, (1, 2, 0, 3)).reshape(9, co, ch)
    ct = jnp.transpose(cotangent, (1, 2, 0))
    groups, tall = ch // 128, hl + 2 * HALO

    half = co // 2
    rows_at = [(hl - HALO, 0)] if ny == 2 else [(hl - HALO, hl - HALO), (0, 0)]
    half_shape = ((9, half, ch), BF16)
    edge_send, first_send = call(
        functools.partial(cut_kernel, rows_at),
        [((len(rows_at), HALO, wl, ch), BF16), half_shape],
        (where, features, first_own),
        [pltpu.SemaphoreType.DMA((1 + len(rows_at),))],
        raw_args=(1, 2),
    )
    second_send, ct_low, ct_high = call(
        cut_later_kernel,
        [half_shape] + [((2, height, co), BF16)] * 2,
        (after(where, edge_send), second_own, ct),
        [pltpu.SemaphoreType.DMA((3,))],
        raw_args=(1, 2),
    )
    up = jnp.transpose(round_y(edge_send[0], 1), (1, 0, 2))
    down = up if ny == 2 else jnp.transpose(round_y(edge_send[1], ny - 1), (1, 0, 2))

    def spread_y(send):
        return jnp.stack([round_y(send, d) for d in range(1, ny)])[:, None]

    first_mine = spread_y(first_send)

    ft = jnp.transpose(after(features, edge_send), (1, 0, 2))
    at = groups * HALO * tall
    shape = ((at + 2 * height * co // 128, 128), BF16)
    if co % 128:
        ct_low, ct_high = ct_low.reshape(-1, 128), ct_high.reshape(-1, 128)
    low, high = call(functools.partial(edge_kernel, dims), [shape] * 2, (where, ft, up, down, ct_low, ct_high))
    left = lax.ppermute(high, "gx", forward)
    right = lax.ppermute(low, "gx", backward)
    first_mine = after(first_mine, left, right)
    first_in = (first_mine, pass_core(first_mine))
    second_mine = spread_y(after(second_send, up))
    second_in = (second_mine, pass_core(second_mine))

    ct = jnp.concatenate([left[at:].reshape(2, height, co), ct, right[at:].reshape(2, height, co)], axis=0)
    if ny == 2:
        window = hl + OFF
        rows_of = lambda y: lax.dynamic_slice_in_dim(ct, y * (height - window), window, 1)
    else:
        ct = jnp.pad(ct, ((0, 0), (OFF, rows - OFF - hl), (0, 0)))
        rows_of = lambda y: lax.dynamic_slice_in_dim(ct, y * hl, rows, 1)
    cot_send = [rows_of((iy + d) % ny) for d in range(1, ny)]
    ft = after(ft, cot_send, second_mine)
    cots = [rows_of(iy)] + [round_y(cot_send[d - 1], d) for d in range(1, ny)]
    if ny != 2:
        full = jnp.zeros((wl + 4, rows, ch), BF16)
        for d, part in enumerate(cots):
            full = lax.dynamic_update_slice_in_dim(full, part, ((iy - d) % ny) * co, 2)
        cots = [full]

    bf = lambda *s: pltpu.VMEM(s, BF16)
    weights = bf(9, ch, ch)

    fbuf_shape = ((wl + 8, rows, ch), BF16)
    hidden, slope1, fbuf = call(
        functools.partial(conv1_kernel, dims),
        [((wl + 6, rows, ch), BF16), ((wl + 2, rows, ch), F32), fbuf_shape],
        (where, ft, left, right, up, down, first_own, *first_in),
        [weights],
    )
    act, slope2, second_all = call(
        functools.partial(conv2_kernel, dims),
        [((wl, hl, ch), BF16), ((wl + 4, rows, ch), F32), ((9, ch, ch), BF16)],
        (where, hidden, second_own, *second_in),
    )
    grad_shapes = [((9, ch, ch // 2), F32), ((9, ch, ch // 2), BF16)]
    shifted = bf(wl * rows, 3 * ch)
    inner, outer, keep1, send1 = call(
        functools.partial(inner_kernel, dims, len(cots)),
        [((wl + 2, rows, ch), BF16), ((wl + 4, rows, ch), BF16)] + grad_shapes,
        (where, second_all, slope2, slope1, fbuf, *cots),
        [shifted],
    )
    keep2, send2 = call(
        functools.partial(second_grad_kernel, dims),
        grad_shapes,
        (where, hidden, outer),
        [shifted],
    )
    parts1 = split_filter(where, keep1, pass_core(send1), nx, ny)
    parts2 = split_filter(where, after(keep2, parts1), pass_core(send2), nx, ny)
    (input_grad,) = call(
        functools.partial(input_kernel, dims),
        [((hl, wl, ch), BF16)],
        (where, inner, first_own, *first_in),
        [weights, pltpu.VMEM((ch // 128, hl * wl, 128), F32)],
    )
    if ny == 2:
        (own1, other1, send1), (own2, other2, send2) = parts1, parts2
        axes, pairs = ("gx", "gy"), [halving_pairs(nx, step) for step in range(2)]
        came1 = lax.ppermute(send1, axes, pairs[0])
        came2 = lax.ppermute(send2, axes, pairs[0])
        came1 = after(came1, parts2, input_grad)
        shape = own1.shape
        own1, pass1 = call(fold_kernel, [(shape, F32), (shape, BF16)], (own1, other1, came1), smem_args=0)
        own2, pass2 = call(fold_kernel, [(shape, F32), (shape, BF16)], (own2, other2, came2), smem_args=0)
        total1 = add([own1, lax.ppermute(pass1, axes, pairs[1])])
        total2 = add([own2, lax.ppermute(pass2, axes, pairs[1])])
    else:
        total1 = add([after(parts1[0], parts2, input_grad)] + send_planes(parts1, nx, ny))
        total2 = add([parts2[0]] + send_planes(parts2, nx, ny))
    act = after(act, total1)

    def channels_of(y):
        return lax.dynamic_slice_in_dim(act, y * co, co, 2)

    parts = [channels_of(iy)] + [round_y(channels_of((iy + d) % ny), d) for d in range(1, ny)]
    output = jnp.zeros((wl, height, co), BF16)
    for d, part in enumerate(parts):
        output = lax.dynamic_update_slice_in_dim(output, part, ((iy - d) % ny) * hl, 1)
    output = jnp.transpose(output, (2, 0, 1))

    for step in range(len(far_bits(nx))):
        other1 = far_partner(total1, step, nx)
        other2 = far_partner(total2, step, nx)
        total1 = add([total1, other1])
        total2 = add([total2, other2])
    total2 = after(total2, output)
    beside1 = lax.ppermute(total1, "gx", [(g, g ^ 2) for g in range(nx)])
    beside2 = lax.ppermute(total2, "gx", [(g, g ^ 2) for g in range(nx)])
    first_grad = finish(where, total1, beside1, nx, ix, scale_factor)
    second_grad = finish(where, total2, beside2, nx, ix, scale_factor)
    return output, input_grad, first_grad, second_grad


def solution(mesh):
    in_specs = (
        P("gy", "gx", None),
        P("gy", None, None, None),
        P("gy", None, None, None),
        P("gy", "gx", None),
    )
    out_specs = (
        P("gy", "gx", None),
        P("gy", "gx", None),
        P("gy", None, None, None),
        P("gy", None, None, None),
    )
    return jax.shard_map(body, mesh=mesh, in_specs=in_specs, out_specs=out_specs, check_vma=False)
```
